32 devices in a mesh: member: 2 (over x), lon: 16 (over z, y, core).
Axes of the slice: x: 2, y: 2, z: 4, core: 2. Of those that a mesh axis runs over, the one named last changes fastest.
Arguments:
- surface_old: float32 [1024, 256], P(('member', 'lon')), parts along dimension 0, may hold values from -6 to 6
- surface_forcing: float32 [1024, 256], P(('member', 'lon')), parts along dimension 0, may hold values from -13 to 13
- surface_coeff: float32 [512, 256], P('lon'), may hold values from 0.1 to 1
- ocean_mask: int32 [512, 256], P('lon'), may hold values from 0 to 1, as said below
- column_depth: int32 [256, 512], P('lon'), may hold values from 0 to 16, as said below
- east_depth: int32 [256, 512], P('lon'), may hold values from 0 to 16, as said below
- tracers: float32 [16, 16, 256, 512], P('member', None, 'lon'), parts along dimension 0, may hold values from 0.05 to 2
- u_clinic: float32 [32, 256, 512], P('member', 'lon'), parts along dimension 0, may hold values from -0.9 to 0.9
- v_clinic: float32 [32, 256, 512], P('member', 'lon'), parts along dimension 0, may hold values from -0.9 to 0.9
Outputs:
- surface: float32 [1024, 256], P(('member', 'lon')), parts along dimension 0
- tracers_new: float32 [16, 16, 256, 512], P('member', None, 'lon'), parts along dimension 0
The draws below stay inside these ranges and needn't reach their ends.
There are 2 independent parts, one for each index of `member`. The reference program is written for one: setup_inputs(seed, part) draws one part's arguments, and reference() takes and returns one part's arrays. A program takes and returns all parts, laid end to end along the dimension named above; an argument that names none is the same for every part. Nothing has to cross between parts.
Inputs may be any that keep to these rules, and one draw needn't show every extreme that they name: ocean_mask[j, i] is 1 exactly where column_depth[i, j] is positive, else 0. `column_depth`: 0 marks land. east_depth[i, j] is the smaller of column_depth[i, j] and column_depth[i + 1, j], longitudes periodic.
All inputs are finite; a program needn't handle non-finite values.
Results may differ from the reference program's by a relative error of at most 0.0003.
Values sent between devices are 32-bit elements; how exact they have to be, the bound alone decides.
A program may use at most 64 MiB of HBM per device.

```python
import math
import jax
import jax.numpy as jnp
from jax import lax

TRACERS = 8
LEVELS = 16
LATITUDES = 512
SOLVER_ITERS = 4
LONGITUDES = 256


def depth_table(key):
    land_key, level_key = jax.random.split(jax.random.fold_in(key, 7))
    is_land = jax.random.randint(land_key, (LONGITUDES, LATITUDES), 0, 4) == 0
    levels_drawn = jax.random.randint(level_key, (LONGITUDES, LATITUDES), 1, LEVELS + 1)
    depths_all = jnp.where(is_land, 0, levels_drawn).astype(jnp.int32)
    depths_all = depths_all.at[0, 0].set(LEVELS).at[1, 0].set(LEVELS).at[2, 0].set(0)
    return depths_all


def draw_column_depth(key, part):
    return depth_table(key)


def draw_east_depth(key, part):
    depths_all = depth_table(key)
    return jnp.minimum(depths_all, jnp.roll(depths_all, -1, axis=0)).astype(jnp.int32)


def draw_ocean_mask(key, part):
    return (depth_table(key) > 0).astype(jnp.int32).T


def draw_surface_forcing(key, part):
    rows_frac = jnp.arange(LATITUDES, dtype=jnp.float32)[:, None] / (LATITUDES - 1)
    normal_part = jnp.clip(jax.random.normal(key, (LATITUDES, LONGITUDES), jnp.float32), -4.0, 4.0)
    return ((1.0 + 2.0 * rows_frac) * normal_part).astype(jnp.float32)


def steps_of(stream_key, shape, cuts, least, high):
    level = 1.0
    for dim, parts in cuts:
        draws = jax.random.uniform(jax.random.fold_in(jax.random.fold_in(stream_key, 6), dim), (parts,), jnp.float32, least / len(cuts), high / len(cuts))
        level = level * jnp.repeat(jnp.exp(draws), shape[dim] // parts).reshape((-1,) + (1,) * (len(shape) - 1 - dim))
    return level


def scatter_about(own_key, shape, deviation, bound, cuts=(), kind=jnp.bfloat16):
    array = deviation * jax.random.normal(own_key, shape, jnp.float32)
    if cuts:
        array = array * steps_of(own_key, shape, cuts, -0.22, 0.18)
    return jnp.clip(array, -bound, bound).astype(kind)


def setup_inputs(seed: int = 0, part: int = 0) -> dict:
    seeds = jax.random.split(jax.random.key(seed), 10)
    own_keys = jax.random.split(jax.random.fold_in(seeds[9], part), 10)
    return {
        "surface_old": scatter_about(own_keys[0], (LATITUDES, LONGITUDES), 1.0, 6.0, ((0, 16),), jnp.float32),
        "surface_forcing": draw_surface_forcing(jax.random.fold_in(jax.random.fold_in(seeds[9], part), 71), part),
        "surface_coeff": jnp.clip(jnp.exp(math.log(1.0) - 2.3025851 * jax.random.uniform(seeds[2], (LATITUDES, LONGITUDES), jnp.float32) ** steps_of(seeds[2], (LATITUDES, LONGITUDES), ((0, 16),), -0.2, 0.2)), 0.1, 1.0),
        "ocean_mask": draw_ocean_mask(jax.random.fold_in(seeds[9], 71), part),
        "column_depth": draw_column_depth(jax.random.fold_in(seeds[9], 71), part),
        "east_depth": draw_east_depth(jax.random.fold_in(seeds[9], 71), part),
        "tracers": jnp.clip(0.05 + 1.95 * jax.random.uniform(own_keys[6], (TRACERS, LEVELS, LONGITUDES, LATITUDES), jnp.float32) ** steps_of(own_keys[6], (TRACERS, LEVELS, LONGITUDES, LATITUDES), ((2, 16),), -0.2, 0.2), 0.05, 2.0),
        "u_clinic": scatter_about(own_keys[7], (LEVELS, LONGITUDES, LATITUDES), 0.3, 0.9, ((1, 16),), jnp.float32),
        "v_clinic": scatter_about(own_keys[8], (LEVELS, LONGITUDES, LATITUDES), 0.3, 0.9, ((1, 16),), jnp.float32),
    }


BARO_GAIN = 0.1
HORIZ_DIFF = 0.1
VERT_DIFF = 0.15
RATE_CARBON = 0.3
RATE_AMMONIUM = 0.2
RATE_NITRITE = 0.2
RATE_SULFIDE = 0.3
RATE_NITROUS = 0.2
HALF_OXYGEN = 0.3
HALF_NITRATE = 0.3
HALF_NITRITE = 0.3
YIELD_NITROUS = 0.3


def apply_operator(values_in, mask_float, coeff):
    masked = mask_float * values_in
    northern = jnp.concatenate([masked[1:], masked[-1:, ::-1]], axis=0)
    southern = jnp.concatenate([jnp.zeros_like(masked[:1]), masked[:-1]], axis=0)
    eastern = jnp.roll(masked, -1, axis=1)
    western = jnp.roll(masked, 1, axis=1)
    return (coeff + 4.0 * mask_float) * values_in - mask_float * (((northern + southern) + eastern) + western)


def solve_surface(right_side, mask_float, coeff):
    solution = jnp.zeros_like(right_side)
    residual = right_side
    direction = right_side
    norm_now = jnp.sum(residual * residual)
    for sweep in range(SOLVER_ITERS):
        applied = apply_operator(direction, mask_float, coeff)
        step_size = norm_now / jnp.sum(direction * applied)
        solution = solution + step_size * direction
        residual = residual - step_size * applied
        norm_next = jnp.sum(residual * residual)
        direction = residual + (norm_next / norm_now) * direction
        norm_now = norm_next
    return solution


def open_faces(column_depth, east_depth, east_baro, north_baro, u_clinic, v_clinic):
    level_index = lax.broadcasted_iota(jnp.int32, u_clinic.shape, 0)
    wet = (level_index < column_depth[None]).astype(jnp.float32)
    east_open = (level_index < east_depth[None]).astype(jnp.float32)
    north_open = wet * jnp.concatenate([wet[:, :, 1:], jnp.zeros_like(wet[:, :, :1])], axis=2)
    below_open = wet * jnp.concatenate([wet[1:], jnp.zeros_like(wet[:1])], axis=0)
    east_flow = (u_clinic + east_baro[None]) * east_open
    north_flow = (v_clinic + north_baro[None]) * north_open
    return wet, east_open, north_open, below_open, east_flow, north_flow


def meridional_vertical(masked, north_flow, north_open, below_open):
    count_rows = masked.shape[-1]
    pad_widths = [(0, 0)] * (masked.ndim - 1) + [(2, 2)]
    padded = jnp.pad(masked, pad_widths)
    south_one = padded[..., 1:count_rows + 1]
    north_one = padded[..., 3:count_rows + 3]
    north_two = padded[..., 4:count_rows + 4]
    face_north = (7.0 * (masked + north_one) - (south_one + north_two)) / 12.0
    flux_north = north_flow * face_north - HORIZ_DIFF * (north_one - masked) * north_open
    flux_south = jnp.concatenate([jnp.zeros_like(flux_north[..., :1]), flux_north[..., :-1]], axis=-1)
    below = jnp.concatenate([masked[..., 1:, :, :], jnp.zeros_like(masked[..., :1, :, :])], axis=-3)
    flux_down = VERT_DIFF * (below - masked) * below_open
    flux_up = jnp.concatenate([jnp.zeros_like(flux_down[..., :1, :, :]), flux_down[..., :-1, :, :]], axis=-3)
    return (flux_south - flux_north) + (flux_down - flux_up)


def redox_sources(masked):
    oxygen = masked[0]
    nitrate = masked[1]
    nitrite = masked[2]
    ammonium = masked[3]
    carbon = masked[5]
    sulfide = masked[6]
    nitrous = masked[7]
    breakdown = RATE_CARBON * carbon
    with_oxygen = oxygen / (oxygen + HALF_OXYGEN)
    with_nitrate = (1.0 - with_oxygen) * nitrate / (nitrate + HALF_NITRATE)
    with_nitrite = (1.0 - with_oxygen - with_nitrate) * nitrite / (nitrite + HALF_NITRITE)
    with_sulfate = 1.0 - with_oxygen - with_nitrate - with_nitrite
    first_nitr = RATE_AMMONIUM * ammonium * with_oxygen
    second_nitr = RATE_NITRITE * nitrite * with_oxygen
    sulfide_ox = RATE_SULFIDE * sulfide * with_oxygen
    return jnp.stack([
        -1.3 * breakdown * with_oxygen - 1.5 * first_nitr - 0.5 * second_nitr - 2.0 * sulfide_ox,
        -0.9 * breakdown * with_nitrate + second_nitr,
        0.9 * breakdown * with_nitrate - 0.6 * breakdown * with_nitrite + (1.0 - YIELD_NITROUS) * first_nitr - second_nitr,
        0.15 * breakdown - first_nitr,
        0.1 * breakdown,
        -breakdown,
        0.5 * breakdown * with_sulfate - sulfide_ox,
        YIELD_NITROUS * first_nitr - RATE_NITROUS * nitrous * (1.0 - with_oxygen),
    ])


def zonal_terms(masked, east_flow, east_open):
    east_one = jnp.roll(masked, -1, axis=-2)
    east_two = jnp.roll(masked, -2, axis=-2)
    west_one = jnp.roll(masked, 1, axis=-2)
    face_east = (7.0 * (masked + east_one) - (west_one + east_two)) / 12.0
    flux_east = east_flow * face_east - HORIZ_DIFF * (east_one - masked) * east_open
    return jnp.roll(flux_east, 1, axis=-2) - flux_east


def reference(surface_old, surface_forcing, surface_coeff, ocean_mask, column_depth, east_depth, tracers, u_clinic, v_clinic):
    mask_float = ocean_mask.astype(jnp.float32)
    right_side = surface_coeff * surface_old + surface_forcing
    surface = solve_surface(right_side, mask_float, surface_coeff)
    band_flow = -BARO_GAIN * (jnp.roll(surface, -1, axis=1) - surface)
    strip_surface = surface.T
    above_surface = jnp.concatenate([strip_surface[:, 1:], strip_surface[:, -1:]], axis=1)
    north_baro = -BARO_GAIN * (above_surface - strip_surface)
    wet, east_open, north_open, below_open, east_flow, north_flow = open_faces(
        column_depth, east_depth, band_flow.T, north_baro, u_clinic, v_clinic)
    masked = tracers * wet[None]

    def per_tracer(single):
        return zonal_terms(single, east_flow, east_open) + meridional_vertical(single, north_flow, north_open, below_open)

    transport = lax.map(per_tracer, masked)
    tendency = transport + redox_sources(masked)
    tracers_new = tracers + wet[None] * tendency
    return surface, tracers_new
```

```python
import jax
import jax.numpy as jnp
from jax import lax
from jax.sharding import PartitionSpec as P

SOLVER_ITERS = 4


BARO_GAIN = 0.1
HORIZ_DIFF = 0.1
VERT_DIFF = 0.15
RATE_CARBON = 0.3
RATE_AMMONIUM = 0.2
RATE_NITRITE = 0.2
RATE_SULFIDE = 0.3
RATE_NITROUS = 0.2
HALF_OXYGEN = 0.3
HALF_NITRATE = 0.3
HALF_NITRITE = 0.3
YIELD_NITROUS = 0.3


def padded_2(block, width):
    low = shifted(block[:, :, -width:], "lon", 1, True)
    high = shifted(block[:, :, :width], "lon", -1, True)
    return low, high


HALO = SOLVER_ITERS
CENTER = 4.55
HALF_WIDTH = 4.45


def shifted(block, axis_name, step, periodic):
    count = lax.axis_size(axis_name)
    pairs = [(i, (i + step) % count) for i in range(count) if periodic or 0 <= i + step < count]
    return lax.ppermute(block, axis_name, pairs)


def extended_band(fields):
    below = shifted(fields[:, -HALO:], "lon", 1, False)
    above = shifted(fields[:, :HALO], "lon", -1, False)
    top_device = lax.axis_index("lon") == lax.axis_size("lon") - 1
    above = jnp.where(top_device, fields[:, -HALO:][:, ::-1, ::-1], above)
    return jnp.concatenate([below, fields, above], axis=1)


def apply_extended(values_in, mask_float, coeff):
    masked = mask_float * values_in
    edge = jnp.zeros_like(masked[:1])
    northern = jnp.concatenate([masked[1:], edge], axis=0)
    southern = jnp.concatenate([edge, masked[:-1]], axis=0)
    eastern = jnp.roll(masked, -1, axis=1)
    western = jnp.roll(masked, 1, axis=1)
    return (coeff + 4.0 * mask_float) * values_in - mask_float * (
        northern + southern + eastern + western
    )


def krylov_basis(extended):
    right_side, coeff, mask_float = extended[0], extended[1], extended[2]
    basis = [right_side]
    for order in range(SOLVER_ITERS):
        now = basis[-1]
        image = (apply_extended(now, mask_float, coeff) - CENTER * now) * (1.0 / HALF_WIDTH)
        basis.append(image if order == 0 else 2.0 * image - basis[-2])
    return [field[HALO:-HALO] for field in basis]


GRAM_PAIRS = [(i, j) for i in range(SOLVER_ITERS) for j in range(i, SOLVER_ITERS + 1)]


def operator_on_coefficients(given):
    out = [CENTER * value for value in given] + [0.0]
    for k, value in enumerate(given):
        if k == 0:
            out[1] = out[1] + HALF_WIDTH * value
        else:
            out[k - 1] = out[k - 1] + 0.5 * HALF_WIDTH * value
            out[k + 1] = out[k + 1] + 0.5 * HALF_WIDTH * value
    return out


def gram_product(gram, left, right):
    total = 0.0
    for i, x in enumerate(left):
        for j, y in enumerate(right):
            total = total + gram[(min(i, j), max(i, j))] * (x * y)
    return total


def added(first, second):
    size = max(len(first), len(second))
    first = list(first) + [0.0] * (size - len(first))
    second = list(second) + [0.0] * (size - len(second))
    return [x + y for x, y in zip(first, second)]


def solver_coefficients(gram):
    one = jnp.ones_like(gram[(0, 0)])
    solution, residual, direction = [], [one], [one]
    norm_now = gram[(0, 0)]
    for sweep in range(SOLVER_ITERS):
        applied = operator_on_coefficients(direction)
        step_size = norm_now / gram_product(gram, direction, applied)
        solution = added(solution, [step_size * x for x in direction])
        if sweep == SOLVER_ITERS - 1:
            break
        residual = added(residual, [-step_size * x for x in applied])
        norm_next = gram_product(gram, residual, residual)
        ratio = norm_next / norm_now
        direction = added(residual, [ratio * x for x in direction])
        norm_now = norm_next
    return solution


def solve_and_hand_over(surface_old, surface_forcing, surface_coeff, ocean_mask):
    rows, columns = surface_old.shape
    count = lax.axis_size("lon")
    width = columns // count
    right_side = surface_coeff * surface_old + surface_forcing
    extended = extended_band(
        jnp.stack([right_side, surface_coeff, ocean_mask.astype(jnp.float32)])
    )
    basis = krylov_basis(extended)
    partial = jnp.stack([jnp.sum(basis[i] * basis[j]) for i, j in GRAM_PAIRS])
    stacked = jnp.stack(basis[:SOLVER_ITERS])
    parts = stacked.reshape(SOLVER_ITERS, rows, count, width)
    west = jnp.roll(parts[..., -1:], 1, axis=2)
    east = jnp.roll(parts[..., :1], -1, axis=2)
    wide = jnp.concatenate([west, parts, east], axis=-1)
    wide = wide.transpose(2, 3, 0, 1).reshape(count, width + 2, SOLVER_ITERS * rows)
    lanes = max(wide.shape[2], 128)
    wide = jnp.pad(wide, ((0, 0), (0, 0), (0, lanes - wide.shape[2])))
    sums = jnp.broadcast_to(
        jnp.pad(partial, (0, lanes - len(GRAM_PAIRS)))[None, None], (count, 1, lanes)
    )
    moved = lax.all_to_all(
        jnp.concatenate([wide, sums], axis=1), "lon", split_axis=0, concat_axis=0, tiled=True
    )
    totals = jnp.sum(moved[:, width + 2], axis=0)
    gram = {pair: totals[n] for n, pair in enumerate(GRAM_PAIRS)}
    weights = solver_coefficients(gram)
    surface = sum(weights[k] * basis[k] for k in range(SOLVER_ITERS))
    strip = sum(
        weights[k] * moved[:, : width + 2, k * rows : (k + 1) * rows] for k in range(SOLVER_ITERS)
    )
    strip = strip.transpose(1, 0, 2).reshape(width + 2, count * rows)
    return surface, strip


def open_faces(column_depth, east_depth, east_baro, north_baro, u_clinic, v_clinic):
    level_index = lax.broadcasted_iota(jnp.int32, u_clinic.shape, 0)
    wet = (level_index < column_depth[None]).astype(jnp.float32)
    east_open = (level_index < east_depth[None]).astype(jnp.float32)
    north_open = wet * jnp.concatenate([wet[:, :, 1:], jnp.zeros_like(wet[:, :, :1])], axis=2)
    below_open = wet * jnp.concatenate([wet[1:], jnp.zeros_like(wet[:1])], axis=0)
    east_flow = (u_clinic + east_baro[None]) * east_open
    north_flow = (v_clinic + north_baro[None]) * north_open
    return (wet, east_open, north_open, below_open, east_flow, north_flow)


def meridional_vertical(masked, north_flow, north_open, below_open):
    count_rows = masked.shape[-1]
    pad_widths = [(0, 0)] * (masked.ndim - 1) + [(2, 2)]
    padded = jnp.pad(masked, pad_widths)
    south_one = padded[..., 1 : count_rows + 1]
    north_one = padded[..., 3 : count_rows + 3]
    north_two = padded[..., 4 : count_rows + 4]
    face_north = (7.0 * (masked + north_one) - (south_one + north_two)) / 12.0
    flux_north = north_flow * face_north - HORIZ_DIFF * (north_one - masked) * north_open
    flux_south = jnp.concatenate(
        [jnp.zeros_like(flux_north[..., :1]), flux_north[..., :-1]], axis=-1
    )
    below = jnp.concatenate([masked[..., 1:, :, :], jnp.zeros_like(masked[..., :1, :, :])], axis=-3)
    flux_down = VERT_DIFF * (below - masked) * below_open
    flux_up = jnp.concatenate(
        [jnp.zeros_like(flux_down[..., :1, :, :]), flux_down[..., :-1, :, :]], axis=-3
    )
    return flux_south - flux_north + (flux_down - flux_up)


def redox_sources(masked):
    oxygen = masked[0]
    nitrate = masked[1]
    nitrite = masked[2]
    ammonium = masked[3]
    carbon = masked[5]
    sulfide = masked[6]
    nitrous = masked[7]
    breakdown = RATE_CARBON * carbon
    with_oxygen = oxygen / (oxygen + HALF_OXYGEN)
    with_nitrate = (1.0 - with_oxygen) * nitrate / (nitrate + HALF_NITRATE)
    with_nitrite = (1.0 - with_oxygen - with_nitrate) * nitrite / (nitrite + HALF_NITRITE)
    with_sulfate = 1.0 - with_oxygen - with_nitrate - with_nitrite
    first_nitr = RATE_AMMONIUM * ammonium * with_oxygen
    second_nitr = RATE_NITRITE * nitrite * with_oxygen
    sulfide_ox = RATE_SULFIDE * sulfide * with_oxygen
    return jnp.stack(
        [
            -1.3 * breakdown * with_oxygen
            - 1.5 * first_nitr
            - 0.5 * second_nitr
            - 2.0 * sulfide_ox,
            -0.9 * breakdown * with_nitrate + second_nitr,
            0.9 * breakdown * with_nitrate
            - 0.6 * breakdown * with_nitrite
            + (1.0 - YIELD_NITROUS) * first_nitr
            - second_nitr,
            0.15 * breakdown - first_nitr,
            0.1 * breakdown,
            -breakdown,
            0.5 * breakdown * with_sulfate - sulfide_ox,
            YIELD_NITROUS * first_nitr - RATE_NITROUS * nitrous * (1.0 - with_oxygen),
        ]
    )


def body(
    surface_old,
    surface_forcing,
    surface_coeff,
    ocean_mask,
    column_depth,
    east_depth,
    tracers,
    u_clinic,
    v_clinic,
):
    surface, wide_strip = solve_and_hand_over(
        surface_old, surface_forcing, surface_coeff, ocean_mask
    )
    strip_surface = wide_strip[1:-1]
    wide_baro = -BARO_GAIN * (wide_strip[1:] - wide_strip[:-1])
    east_baro = wide_baro[1:]
    above_surface = jnp.concatenate([strip_surface[:, 1:], strip_surface[:, -1:]], axis=1)
    north_baro = -BARO_GAIN * (above_surface - strip_surface)
    wet, east_open, north_open, below_open, east_flow, north_flow = open_faces(
        column_depth, east_depth, east_baro, north_baro, u_clinic, v_clinic
    )
    masked = tracers * wet[None]
    columns_here = masked.shape[2]
    low, high = padded_2(masked, 2)
    tracer_pad = jnp.concatenate([low, masked, high], axis=2)
    west_u = shifted(u_clinic[:, -1:], "lon", 1, True)
    west_open = shifted(east_open[:, -1:], "lon", 1, True)
    west_flow = (west_u + wide_baro[None, :1]) * west_open
    flow_all = jnp.concatenate([west_flow, east_flow], axis=1)
    open_all = jnp.concatenate([west_open, east_open], axis=1)
    center = tracer_pad[:, :, 1 : columns_here + 2]
    east_one = tracer_pad[:, :, 2 : columns_here + 3]
    west_one = tracer_pad[:, :, 0 : columns_here + 1]
    east_two = tracer_pad[:, :, 3 : columns_here + 4]
    face_east = (7.0 * (center + east_one) - (west_one + east_two)) / 12.0
    flux_all = flow_all[None] * face_east - HORIZ_DIFF * (east_one - center) * open_all[None]
    conv_east = flux_all[:, :, :-1] - flux_all[:, :, 1:]
    transport = conv_east + meridional_vertical(
        masked, north_flow[None], north_open[None], below_open[None]
    )
    tendency = transport + redox_sources(masked)
    tracers_new = tracers + wet[None] * tendency
    return (surface, tracers_new)


def solution(mesh):
    in_specs = (
        P(("member", "lon"), None),
        P(("member", "lon"), None),
        P("lon", None),
        P("lon", None),
        P("lon", None),
        P("lon", None),
        P("member", None, "lon", None),
        P("member", "lon", None),
        P("member", "lon", None),
    )
    out_specs = (P(("member", "lon"), None), P("member", None, "lon", None))
    return jax.shard_map(body, mesh=mesh, in_specs=in_specs, out_specs=out_specs, check_vma=False)
```

```python
import jax
import jax.numpy as jnp
from jax import lax
from jax.experimental import pallas as pl
from jax.experimental.pallas import tpu as pltpu
from jax.sharding import PartitionSpec as P

SOLVER_ITERS = 4
TRACERS = 8


BARO_GAIN = 0.1
HORIZ_DIFF = 0.1
VERT_DIFF = 0.15
RATE_CARBON = 0.3
RATE_AMMONIUM = 0.2
RATE_NITRITE = 0.2
RATE_SULFIDE = 0.3
RATE_NITROUS = 0.2
HALF_OXYGEN = 0.3
HALF_NITRATE = 0.3
HALF_NITRITE = 0.3
YIELD_NITROUS = 0.3


HALO = SOLVER_ITERS
CENTER = 4.55
HALF_WIDTH = 4.45
LANES = 128
RING = 24
WIDTH = 16
SUM_ROW = WIDTH + 1


def shifted(block, axis_name, step, periodic):
    count = lax.axis_size(axis_name)
    pairs = [(i, (i + step) % count) for i in range(count) if periodic or 0 <= i + step < count]
    return lax.ppermute(block, axis_name, pairs)


def extended_band(fields):
    below = shifted(fields[:, -HALO:], "lon", 1, False)
    above = shifted(fields[:, :HALO], "lon", -1, False)
    top_device = lax.axis_index("lon") == lax.axis_size("lon") - 1
    above = jnp.where(top_device, fields[:, -HALO:][:, ::-1, ::-1], above)
    return jnp.concatenate([below, fields, above], axis=1)


def apply_extended(values_in, mask_float, coeff):
    masked = mask_float * values_in
    edge = jnp.zeros_like(masked[:1])
    northern = jnp.concatenate([masked[1:], edge], axis=0)
    southern = jnp.concatenate([edge, masked[:-1]], axis=0)
    eastern = jnp.roll(masked, -1, axis=1)
    western = jnp.roll(masked, 1, axis=1)
    return (coeff + 4.0 * mask_float) * values_in - mask_float * (
        northern + southern + eastern + western
    )


def krylov_basis(extended):
    right_side, coeff, mask_float = extended[0], extended[1], extended[2]
    basis = [right_side]
    for order in range(SOLVER_ITERS):
        now = basis[-1]
        image = (apply_extended(now, mask_float, coeff) - CENTER * now) * (1.0 / HALF_WIDTH)
        basis.append(image if order == 0 else 2.0 * image - basis[-2])
    return [field[HALO:-HALO] for field in basis]


GRAM_PAIRS = [(i, j) for i in range(SOLVER_ITERS) for j in range(i, SOLVER_ITERS + 1)]


def operator_on_coefficients(given):
    out = [CENTER * value for value in given] + [0.0]
    for k, value in enumerate(given):
        if k == 0:
            out[1] = out[1] + HALF_WIDTH * value
        else:
            out[k - 1] = out[k - 1] + 0.5 * HALF_WIDTH * value
            out[k + 1] = out[k + 1] + 0.5 * HALF_WIDTH * value
    return out


def gram_product(gram, left, right):
    total = 0.0
    for i, x in enumerate(left):
        for j, y in enumerate(right):
            total = total + gram[(min(i, j), max(i, j))] * (x * y)
    return total


def added(first, second):
    size = max(len(first), len(second))
    first = list(first) + [0.0] * (size - len(first))
    second = list(second) + [0.0] * (size - len(second))
    return [x + y for x, y in zip(first, second)]


def solver_coefficients(gram):
    one = gram[(0, 0)] * 0.0 + 1.0
    solution, residual, direction = [], [one], [one]
    norm_now = gram[(0, 0)]
    for sweep in range(SOLVER_ITERS):
        applied = operator_on_coefficients(direction)
        step_size = norm_now / gram_product(gram, direction, applied)
        solution = added(solution, [step_size * x for x in direction])
        if sweep == SOLVER_ITERS - 1:
            break
        residual = added(residual, [-step_size * x for x in applied])
        norm_next = gram_product(gram, residual, residual)
        ratio = norm_next / norm_now
        direction = added(residual, [ratio * x for x in direction])
        norm_now = norm_next
    return solution


def solve_and_hand_over(surface_old, surface_forcing, surface_coeff, ocean_mask):
    rows, columns = surface_old.shape
    count = lax.axis_size("lon")
    width = columns // count
    right_side = surface_coeff * surface_old + surface_forcing
    extended = extended_band(
        jnp.stack([right_side, surface_coeff, ocean_mask.astype(jnp.float32)])
    )
    basis = krylov_basis(extended)
    partial = jnp.stack([jnp.sum(basis[i] * basis[j]) for i, j in GRAM_PAIRS])
    stacked = jnp.stack(basis[:SOLVER_ITERS])
    parts = stacked.reshape(SOLVER_ITERS, rows, count, width)
    west = jnp.roll(parts[..., -1:], 1, axis=2)
    east = jnp.roll(parts[..., :1], -1, axis=2)
    wide = jnp.concatenate([west, parts, east], axis=-1)
    wide = wide.transpose(2, 3, 0, 1).reshape(count, width + 2, SOLVER_ITERS * rows)
    wide = jnp.tile(wide, (1, 1, LANES // wide.shape[2]))
    sums = jnp.broadcast_to(
        jnp.pad(partial, (0, LANES - len(GRAM_PAIRS)))[None, None], (count, 1, LANES)
    )
    spare = jnp.zeros((count, RING - width - 3, LANES), jnp.float32)
    payload = jnp.concatenate([wide[:, 1:], sums, spare, wide[:, :1]], axis=1)
    moved = lax.all_to_all(payload, "lon", split_axis=0, concat_axis=0, tiled=True)
    return pl.pallas_call(
        combine_kernel,
        out_shape=(
            jax.ShapeDtypeStruct((rows, columns), jnp.float32),
            jax.ShapeDtypeStruct((RING, rows * count), jnp.float32),
        ),
    )(moved, stacked)


def combine(moved, basis, surface_ref, strip_ref):
    count, rows = moved.shape[0], basis.shape[1]
    totals = jnp.sum(moved[:, SUM_ROW : SUM_ROW + 1, :], axis=0)
    gram = {pair: totals[:, n : n + 1] for n, pair in enumerate(GRAM_PAIRS)}
    weights = solver_coefficients(gram)
    surface_ref[...] = sum(weights[k] * basis[k] for k in range(SOLVER_ITERS))
    lane = lax.broadcasted_iota(jnp.int32, (1, LANES), 1)
    which = (lane // rows) % SOLVER_ITERS
    scale = jnp.zeros((1, LANES), jnp.float32)
    for k in range(SOLVER_ITERS):
        scale = jnp.where(which == k, weights[k], scale)
    slot = jnp.broadcast_to(lane // rows, (RING, LANES))
    per_group = LANES // rows
    for group in range(count // per_group):
        joined = jnp.zeros((RING, LANES), jnp.float32)
        for q in range(per_group):
            scaled = moved[group * per_group + q] * scale
            scaled = scaled + pltpu.roll(scaled, 2 * rows, 1)
            scaled = scaled + pltpu.roll(scaled, rows, 1)
            joined = jnp.where(slot == q, scaled, joined)
        strip_ref[:, group * LANES : (group + 1) * LANES] = joined


def combine_kernel(moved_ref, basis_ref, surface_ref, strip_ref):
    combine(moved_ref, basis_ref, surface_ref, strip_ref)


def redox_sources(masked):
    oxygen = masked[0]
    nitrate = masked[1]
    nitrite = masked[2]
    ammonium = masked[3]
    carbon = masked[5]
    sulfide = masked[6]
    nitrous = masked[7]
    breakdown = RATE_CARBON * carbon
    with_oxygen = oxygen / (oxygen + HALF_OXYGEN)
    with_nitrate = (1.0 - with_oxygen) * nitrate / (nitrate + HALF_NITRATE)
    with_nitrite = (1.0 - with_oxygen - with_nitrate) * nitrite / (nitrite + HALF_NITRITE)
    with_sulfate = 1.0 - with_oxygen - with_nitrate - with_nitrite
    first_nitr = RATE_AMMONIUM * ammonium * with_oxygen
    second_nitr = RATE_NITRITE * nitrite * with_oxygen
    sulfide_ox = RATE_SULFIDE * sulfide * with_oxygen
    return (
        [
            -1.3 * breakdown * with_oxygen
            - 1.5 * first_nitr
            - 0.5 * second_nitr
            - 2.0 * sulfide_ox,
            -0.9 * breakdown * with_nitrate + second_nitr,
            0.9 * breakdown * with_nitrate
            - 0.6 * breakdown * with_nitrite
            + (1.0 - YIELD_NITROUS) * first_nitr
            - second_nitr,
            0.15 * breakdown - first_nitr,
            0.1 * breakdown,
            -breakdown,
            0.5 * breakdown * with_sulfate - sulfide_ox,
            YIELD_NITROUS * first_nitr - RATE_NITROUS * nitrous * (1.0 - with_oxygen),
        ]
    )


def transport_kernel(
    strip_ref, depth_ref, east_depth_ref, u_ref, v_ref, edge_ref, tracers_ref, out_ref
):
    z = pl.program_id(0)
    levels = pl.num_programs(0)
    latitudes = depth_ref.shape[1]
    shape = depth_ref.shape

    def ring(block, shift):
        return pltpu.roll(block, shift % RING, 0)

    def along(block, shift):
        return pltpu.roll(block, shift % latitudes, 1)

    column = lax.broadcasted_iota(jnp.int32, shape, 1)
    depth = depth_ref[...]
    is_wet = depth > z
    wet = is_wet.astype(jnp.float32)
    below = depth > z + 1
    above = jnp.logical_and(is_wet, z > 0)
    strip = strip_ref[...]
    own = strip[: shape[0]]
    flow_edge = edge_ref[TRACERS, 0]
    east_depth = jnp.concatenate(
        [east_depth_ref[...].astype(jnp.float32), ring_edge(flow_edge)], axis=0
    )
    east_open = (east_depth > z.astype(jnp.float32)).astype(jnp.float32)
    u_ext = jnp.concatenate([u_ref[0], flow_edge], axis=0)
    east_flow = (u_ext - BARO_GAIN * (ring(strip, -1) - strip)) * east_open * (1.0 / 12.0)
    east_mix = HORIZ_DIFF * east_open
    last = column == latitudes - 1
    north_open = jnp.where(last, 0.0, wet * along(wet, -1))
    north_flow = (v_ref[0] - BARO_GAIN * (along(own, -1) - own)) * north_open * (1.0 / 12.0)
    north_mix = HORIZ_DIFF * north_open
    first = column == 0
    z_down = jnp.minimum(z + 1, levels - 1)
    z_up = jnp.maximum(z - 1, 0)

    masked_all = []
    transport = []
    for k in range(TRACERS):
        raw = tracers_ref[k, z]
        masked = raw * wet
        masked_all.append(masked)
        extended = jnp.concatenate([masked, edge_ref[k, 0]], axis=0)
        east_one = ring(extended, -1)
        pair = extended + east_one
        face = 8.0 * pair - (ring(pair, 1) + ring(pair, -1))
        flux = east_flow * face - east_mix * (east_one - extended)
        change = (ring(flux, 1) - flux)[: shape[0]]
        north_one = jnp.where(last, 0.0, along(masked, -1))
        pair = masked + north_one
        south_pair = jnp.where(first, masked, along(pair, 1))
        north_pair = jnp.where(last, 0.0, along(pair, -1))
        face = 8.0 * pair - (south_pair + north_pair)
        flux = north_flow * face - north_mix * (north_one - masked)
        change = change + (along(flux, 1) - flux)
        down = jnp.where(below, tracers_ref[k, z_down] - raw, 0.0)
        up = jnp.where(above, raw - tracers_ref[k, z_up], 0.0)
        out_ref[k, 0] = raw + wet * (change + VERT_DIFF * (down - up))
    sources = redox_sources(masked_all)
    for k in range(TRACERS):
        out_ref[k, 0] += wet * sources[k]


def ring_edge(flow_edge):
    return pltpu.roll(flow_edge, 1, 0)


def transport(strip, column_depth, east_depth, u_clinic, v_clinic, edges, tracers):
    count, levels, width, latitudes = tracers.shape
    whole = lambda shape: pl.BlockSpec(shape, lambda z: (0,) * len(shape))
    level = lambda rows: pl.BlockSpec((1, rows, latitudes), lambda z: (z, 0, 0))
    return pl.pallas_call(
        transport_kernel,
        grid=(levels,),
        in_specs=[
            whole(strip.shape),
            whole(column_depth.shape),
            whole(east_depth.shape),
            level(width),
            level(width),
            pl.BlockSpec((count + 1, 1, RING - width, latitudes), lambda z: (0, z, 0, 0)),
            whole(tracers.shape),
        ],
        out_specs=pl.BlockSpec((count, 1, width, latitudes), lambda z: (0, z, 0, 0)),
        out_shape=jax.ShapeDtypeStruct(tracers.shape, jnp.float32),
        compiler_params=pltpu.CompilerParams(vmem_limit_bytes=40 * 2**20),
    )(strip, column_depth, east_depth, u_clinic, v_clinic, edges, tracers)


def edge_blocks(column_depth, east_depth, u_clinic, tracers):
    levels = tracers.shape[1]
    index = lax.broadcasted_iota(jnp.int32, (levels, 1, 1), 0)

    def masked(where):
        wet = index < column_depth[None, where]
        return jnp.where(wet[None], tracers[:, :, where], 0.0)

    ends = jnp.broadcast_to(east_depth[None, -1:].astype(jnp.float32), u_clinic[:, -1:].shape)
    flow = jnp.concatenate([ends, u_clinic[:, -1:]], axis=1)
    low = jnp.concatenate([masked(slice(-2, None)), flow[None]], axis=0)
    low = shifted(low, "lon", 1, True)
    high = shifted(masked(slice(0, 2)), "lon", -1, True)
    high = jnp.pad(high, ((0, 1), (0, 0), (0, RING - WIDTH - 4), (0, 0)))
    return jnp.concatenate([high, low], axis=2)


def body(
    surface_old,
    surface_forcing,
    surface_coeff,
    ocean_mask,
    column_depth,
    east_depth,
    tracers,
    u_clinic,
    v_clinic,
):
    surface, strip = solve_and_hand_over(
        surface_old, surface_forcing, surface_coeff, ocean_mask
    )
    edges = edge_blocks(column_depth, east_depth, u_clinic, tracers)
    tracers_new = transport(
        strip, column_depth, east_depth, u_clinic, v_clinic, edges, tracers
    )
    return (surface, tracers_new)


def solution(mesh):
    in_specs = (
        P(("member", "lon"), None),
        P(("member", "lon"), None),
        P("lon", None),
        P("lon", None),
        P("lon", None),
        P("lon", None),
        P("member", None, "lon", None),
        P("member", "lon", None),
        P("member", "lon", None),
    )
    out_specs = (P(("member", "lon"), None), P("member", None, "lon", None))
    return jax.shard_map(body, mesh=mesh, in_specs=in_specs, out_specs=out_specs, check_vma=False)
```

```python
import jax
import jax.numpy as jnp
from jax import lax
from jax.experimental import pallas as pl
from jax.experimental.pallas import tpu as pltpu
from jax.sharding import PartitionSpec as P

SOLVER_ITERS = 4
TRACERS = 8


BARO_GAIN = 0.1
HORIZ_DIFF = 0.1
VERT_DIFF = 0.15
RATE_CARBON = 0.3
RATE_AMMONIUM = 0.2
RATE_NITRITE = 0.2
RATE_SULFIDE = 0.3
RATE_NITROUS = 0.2
HALF_OXYGEN = 0.3
HALF_NITRATE = 0.3
HALF_NITRITE = 0.3
YIELD_NITROUS = 0.3


HALO = 8
CENTER = 4.55
HALF_WIDTH = 4.45
LANES = 128
RING = 24
WIDTH = 16
SUM_ROW = WIDTH + 1


def apply_extended(values_in, mask_float, diagonal):
    masked = mask_float * values_in
    total, columns = masked.shape
    northern = pltpu.roll(masked, total - 1, 0)
    southern = pltpu.roll(masked, 1, 0)
    eastern = pltpu.roll(masked, columns - 1, 1)
    western = pltpu.roll(masked, 1, 1)
    return diagonal * values_in - mask_float * (northern + southern + eastern + western)


def krylov_basis(right_side, coeff, mask_float):
    diagonal = (coeff + 4.0 * mask_float) - CENTER
    basis = [right_side]
    for order in range(SOLVER_ITERS):
        now = basis[-1]
        image = apply_extended(now, mask_float, diagonal) * (1.0 / HALF_WIDTH)
        basis.append(image if order == 0 else 2.0 * image - basis[-2])
    return [field[HALO:-HALO] for field in basis]


def reversed_both(block):
    for axis in range(2):
        size = block.shape[axis]
        index = lax.broadcasted_iota(jnp.int32, block.shape, axis)
        bit = 1
        while bit < size:
            up = pltpu.roll(block, size - bit, axis)
            down = pltpu.roll(block, bit, axis)
            block = jnp.where((index // bit) % 2 == 0, up, down)
            bit *= 2
    return block


GRAM_PAIRS = [(i, j) for i in range(SOLVER_ITERS) for j in range(i, SOLVER_ITERS + 1)]


def operator_on_coefficients(given):
    out = [CENTER * value for value in given] + [0.0]
    for k, value in enumerate(given):
        if k == 0:
            out[1] = out[1] + HALF_WIDTH * value
        else:
            out[k - 1] = out[k - 1] + 0.5 * HALF_WIDTH * value
            out[k + 1] = out[k + 1] + 0.5 * HALF_WIDTH * value
    return out


def gram_product(gram, left, right):
    total = 0.0
    for i, x in enumerate(left):
        for j, y in enumerate(right):
            total = total + gram[(min(i, j), max(i, j))] * (x * y)
    return total


def added(first, second):
    size = max(len(first), len(second))
    first = list(first) + [0.0] * (size - len(first))
    second = list(second) + [0.0] * (size - len(second))
    return [x + y for x, y in zip(first, second)]


def solver_coefficients(gram):
    one = gram[(0, 0)] * 0.0 + 1.0
    solution, residual, direction = [], [one], [one]
    norm_now = gram[(0, 0)]
    for sweep in range(SOLVER_ITERS):
        applied = operator_on_coefficients(direction)
        step_size = norm_now / gram_product(gram, direction, applied)
        solution = added(solution, [step_size * x for x in direction])
        if sweep == SOLVER_ITERS - 1:
            break
        residual = added(residual, [-step_size * x for x in applied])
        norm_next = gram_product(gram, residual, residual)
        ratio = norm_next / norm_now
        direction = added(residual, [ratio * x for x in direction])
        norm_now = norm_next
    return solution


def solve_kernel(
    old_ref, forcing_ref, coeff_ref, mask_ref, low_ref, high_ref,
    surface_ref, strip_ref, low_out, high_out,
    fields, below_in, above_in, send, recv, basis_kept,
    edge_sems, band_sems, send_sems, recv_sems,
):
    count = lax.axis_size("lon")
    me = lax.axis_index("lon")
    right, left = lax.rem(me + 1, count), lax.rem(me + count - 1, count)
    rows, columns = old_ref.shape
    mesh_id = pl.DeviceIdType.MESH

    barrier = pltpu.get_barrier_semaphore()

    def greet(step, carry):
        other = lax.rem(me + step, count)
        pl.semaphore_signal(barrier, inc=1, device_id={"lon": other}, device_id_type=mesh_id)
        return carry

    lax.fori_loop(1, count, greet, 0)
    fields[0] = coeff_ref[...] * old_ref[...] + forcing_ref[...]
    fields[1] = coeff_ref[...]
    fields[2] = mask_ref[...].astype(jnp.float32)
    pl.semaphore_wait(barrier, count - 1)

    def remote(source, target, sems, n, device):
        return pltpu.make_async_remote_copy(
            src_ref=source,
            dst_ref=target,
            send_sem=sems.at[n, 0],
            recv_sem=sems.at[n, 1],
            device_id={"lon": device},
            device_id_type=mesh_id,
        )

    copies = [
        remote(fields.at[:, rows - HALO :], below_in, band_sems, 0, right),
        remote(fields.at[:, :HALO], above_in, band_sems, 1, left),
        remote(low_ref, low_out, edge_sems, 0, right),
        remote(high_ref, high_out, edge_sems, 1, left),
    ]
    for copy in copies:
        copy.start()
    mirrored = [reversed_both(fields[n, rows - HALO :]) for n in range(3)]
    copies[0].wait()
    copies[1].wait()
    bottom = me == 0
    top = me == count - 1
    extended = [
        jnp.concatenate(
            [
                jnp.where(bottom, 0.0, below_in[n]),
                fields[n],
                jnp.where(top, mirrored[n], above_in[n]),
            ],
            axis=0,
        )
        for n in range(3)
    ]
    basis = krylov_basis(*extended)
    lane = lax.broadcasted_iota(jnp.int32, (1, LANES), 1)
    sums = jnp.zeros((1, LANES), jnp.float32)
    for n, (i, j) in enumerate(GRAM_PAIRS):
        total = jnp.sum(jnp.sum(basis[i] * basis[j], axis=0, keepdims=True), axis=1, keepdims=True)
        sums = jnp.where(lane == n, total, sums)
    for k in range(SOLVER_ITERS):
        basis_kept[k] = basis[k]
    tall = jnp.concatenate(basis[:SOLVER_ITERS] * (LANES // (SOLVER_ITERS * rows)), axis=0)
    turned = jnp.transpose(tall)
    row = lax.broadcasted_iota(jnp.int32, (RING - WIDTH, LANES), 0)
    for d in range(count):
        send[d, :WIDTH] = turned[d * WIDTH : (d + 1) * WIDTH]
        after = (d + 1) % count * WIDTH
        before = (d * WIDTH - 8) % columns
        tail = jnp.where(row == SUM_ROW - WIDTH, sums, turned[after : after + 8])
        send[d, WIDTH:] = jnp.where(row == 7, turned[before : before + 8], tail)

    def block_copy(step):
        other = lax.rem(me + step, count)
        return pltpu.make_async_remote_copy(
            src_ref=send.at[other],
            dst_ref=recv.at[me],
            send_sem=send_sems.at[step],
            recv_sem=recv_sems.at[step],
            device_id={"lon": other},
            device_id_type=mesh_id,
        )

    def start_block(step, carry):
        block_copy(step).start()
        return carry

    def wait_block(step, carry):
        block_copy(step).wait()
        return carry

    lax.fori_loop(1, count, start_block, 0)
    recv[me] = send[me]
    lax.fori_loop(1, count, wait_block, 0)
    combine(recv, basis_kept, surface_ref, strip_ref)
    copies[2].wait()
    copies[3].wait()


def solve_and_hand_over(surface_old, surface_forcing, surface_coeff, ocean_mask, low, high):
    rows, columns = surface_old.shape
    count = lax.axis_size("lon")
    vmem = pl.BlockSpec(memory_space=pltpu.VMEM)
    anywhere = pl.BlockSpec(memory_space=pl.ANY)
    return pl.pallas_call(
        solve_kernel,
        in_specs=[vmem] * 4 + [anywhere] * 2,
        out_specs=[vmem] * 2 + [anywhere] * 2,
        out_shape=(
            jax.ShapeDtypeStruct((rows, columns), jnp.float32),
            jax.ShapeDtypeStruct((RING, rows * count), jnp.float32),
            jax.ShapeDtypeStruct(low.shape, jnp.float32),
            jax.ShapeDtypeStruct(high.shape, jnp.float32),
        ),
        scratch_shapes=[
            pltpu.VMEM((3, rows, columns), jnp.float32),
            pltpu.VMEM((3, HALO, columns), jnp.float32),
            pltpu.VMEM((3, HALO, columns), jnp.float32),
            pltpu.VMEM((count, RING, LANES), jnp.float32),
            pltpu.VMEM((count, RING, LANES), jnp.float32),
            pltpu.VMEM((SOLVER_ITERS, rows, columns), jnp.float32),
            pltpu.SemaphoreType.DMA((2, 2)),
            pltpu.SemaphoreType.DMA((2, 2)),
            pltpu.SemaphoreType.DMA((count,)),
            pltpu.SemaphoreType.DMA((count,)),
        ],
        compiler_params=pltpu.CompilerParams(
            collective_id=0, has_side_effects=True, vmem_limit_bytes=8 * 2**20
        ),
    )(surface_old, surface_forcing, surface_coeff, ocean_mask, low, high)


def combine(moved, basis, surface_ref, strip_ref):
    count, rows = moved.shape[0], basis.shape[1]
    totals = moved[0, SUM_ROW : SUM_ROW + 1, :]
    for source in range(1, count):
        totals = totals + moved[source, SUM_ROW : SUM_ROW + 1, :]
    gram = {pair: totals[:, n : n + 1] for n, pair in enumerate(GRAM_PAIRS)}
    weights = solver_coefficients(gram)
    surface_ref[...] = sum(weights[k] * basis[k] for k in range(SOLVER_ITERS))
    lane = lax.broadcasted_iota(jnp.int32, (1, LANES), 1)
    which = (lane // rows) % SOLVER_ITERS
    scale = jnp.zeros((1, LANES), jnp.float32)
    for k in range(SOLVER_ITERS):
        scale = jnp.where(which == k, weights[k], scale)
    slot = jnp.broadcast_to(lane // rows, (RING, LANES))
    per_group = LANES // rows
    for group in range(count // per_group):
        joined = jnp.zeros((RING, LANES), jnp.float32)
        for q in range(per_group):
            scaled = moved[group * per_group + q] * scale
            scaled = scaled + pltpu.roll(scaled, 2 * rows, 1)
            scaled = scaled + pltpu.roll(scaled, rows, 1)
            joined = jnp.where(slot == q, scaled, joined)
        strip_ref[:, group * LANES : (group + 1) * LANES] = joined


def redox_sources(masked):
    oxygen = masked[0]
    nitrate = masked[1]
    nitrite = masked[2]
    ammonium = masked[3]
    carbon = masked[5]
    sulfide = masked[6]
    nitrous = masked[7]
    breakdown = RATE_CARBON * carbon
    with_oxygen = oxygen / (oxygen + HALF_OXYGEN)
    with_nitrate = (1.0 - with_oxygen) * nitrate / (nitrate + HALF_NITRATE)
    with_nitrite = (1.0 - with_oxygen - with_nitrate) * nitrite / (nitrite + HALF_NITRITE)
    with_sulfate = 1.0 - with_oxygen - with_nitrate - with_nitrite
    first_nitr = RATE_AMMONIUM * ammonium * with_oxygen
    second_nitr = RATE_NITRITE * nitrite * with_oxygen
    sulfide_ox = RATE_SULFIDE * sulfide * with_oxygen
    return (
        [
            -1.3 * breakdown * with_oxygen
            - 1.5 * first_nitr
            - 0.5 * second_nitr
            - 2.0 * sulfide_ox,
            -0.9 * breakdown * with_nitrate + second_nitr,
            0.9 * breakdown * with_nitrate
            - 0.6 * breakdown * with_nitrite
            + (1.0 - YIELD_NITROUS) * first_nitr
            - second_nitr,
            0.15 * breakdown - first_nitr,
            0.1 * breakdown,
            -breakdown,
            0.5 * breakdown * with_sulfate - sulfide_ox,
            YIELD_NITROUS * first_nitr - RATE_NITROUS * nitrous * (1.0 - with_oxygen),
        ]
    )


def transport_kernel(
    strip_ref, depth_ref, east_depth_ref, u_ref, v_ref, edge_ref, tracers_ref, out_ref
):
    z = pl.program_id(0)
    levels = pl.num_programs(0)
    latitudes = depth_ref.shape[1]
    shape = depth_ref.shape

    def ring(block, shift):
        return pltpu.roll(block, shift % RING, 0)

    def along(block, shift):
        return pltpu.roll(block, shift % latitudes, 1)

    column = lax.broadcasted_iota(jnp.int32, shape, 1)
    depth = depth_ref[...]
    is_wet = depth > z
    wet = is_wet.astype(jnp.float32)
    below = depth > z + 1
    above = jnp.logical_and(is_wet, z > 0)
    strip = strip_ref[...]
    own = strip[: shape[0]]
    flow_edge = edge_ref[TRACERS, 0]
    east_depth = jnp.concatenate(
        [east_depth_ref[...].astype(jnp.float32), ring_edge(flow_edge)], axis=0
    )
    east_open = (east_depth > z.astype(jnp.float32)).astype(jnp.float32)
    u_ext = jnp.concatenate([u_ref[0], flow_edge], axis=0)
    east_flow = (u_ext - BARO_GAIN * (ring(strip, -1) - strip)) * east_open * (1.0 / 12.0)
    east_mix = HORIZ_DIFF * east_open
    last = column == latitudes - 1
    north_open = jnp.where(last, 0.0, wet * along(wet, -1))
    north_flow = (v_ref[0] - BARO_GAIN * (along(own, -1) - own)) * north_open * (1.0 / 12.0)
    north_mix = HORIZ_DIFF * north_open
    first = column == 0
    z_down = jnp.minimum(z + 1, levels - 1)
    z_up = jnp.maximum(z - 1, 0)

    masked_all = []
    transport = []
    for k in range(TRACERS):
        raw = tracers_ref[k, z]
        masked = raw * wet
        masked_all.append(masked)
        extended = jnp.concatenate([masked, edge_ref[k, 0]], axis=0)
        east_one = ring(extended, -1)
        pair = extended + east_one
        face = 8.0 * pair - (ring(pair, 1) + ring(pair, -1))
        flux = east_flow * face - east_mix * (east_one - extended)
        change = (ring(flux, 1) - flux)[: shape[0]]
        north_one = jnp.where(last, 0.0, along(masked, -1))
        pair = masked + north_one
        south_pair = jnp.where(first, masked, along(pair, 1))
        north_pair = jnp.where(last, 0.0, along(pair, -1))
        face = 8.0 * pair - (south_pair + north_pair)
        flux = north_flow * face - north_mix * (north_one - masked)
        change = change + (along(flux, 1) - flux)
        down = jnp.where(below, tracers_ref[k, z_down] - raw, 0.0)
        up = jnp.where(above, raw - tracers_ref[k, z_up], 0.0)
        out_ref[k, 0] = raw + wet * (change + VERT_DIFF * (down - up))
    sources = redox_sources(masked_all)
    for k in range(TRACERS):
        out_ref[k, 0] += wet * sources[k]


def ring_edge(flow_edge):
    return pltpu.roll(flow_edge, 1, 0)


def transport(strip, column_depth, east_depth, u_clinic, v_clinic, edges, tracers):
    count, levels, width, latitudes = tracers.shape
    whole = lambda shape: pl.BlockSpec(shape, lambda z: (0,) * len(shape))
    level = lambda rows: pl.BlockSpec((1, rows, latitudes), lambda z: (z, 0, 0))
    return pl.pallas_call(
        transport_kernel,
        grid=(levels,),
        in_specs=[
            whole(strip.shape),
            whole(column_depth.shape),
            whole(east_depth.shape),
            level(width),
            level(width),
            pl.BlockSpec((count + 1, 1, RING - width, latitudes), lambda z: (0, z, 0, 0)),
            whole(tracers.shape),
        ],
        out_specs=pl.BlockSpec((count, 1, width, latitudes), lambda z: (0, z, 0, 0)),
        out_shape=jax.ShapeDtypeStruct(tracers.shape, jnp.float32),
        compiler_params=pltpu.CompilerParams(vmem_limit_bytes=40 * 2**20),
    )(strip, column_depth, east_depth, u_clinic, v_clinic, edges, tracers)


def edge_blocks(column_depth, east_depth, u_clinic, tracers):
    levels = tracers.shape[1]
    index = lax.broadcasted_iota(jnp.int32, (levels, 1, 1), 0)

    def masked(where):
        wet = index < column_depth[None, where]
        return jnp.where(wet[None], tracers[:, :, where], 0.0)

    ends = jnp.broadcast_to(east_depth[None, -1:].astype(jnp.float32), u_clinic[:, -1:].shape)
    flow = jnp.concatenate([ends, u_clinic[:, -1:]], axis=1)
    low = jnp.concatenate([masked(slice(-2, None)), flow[None]], axis=0)
    return low, masked(slice(0, 2))


def ring_of(low, high):
    high = jnp.pad(high, ((0, 1), (0, 0), (0, RING - WIDTH - 4), (0, 0)))
    return jnp.concatenate([high, low], axis=2)


def body(
    surface_old,
    surface_forcing,
    surface_coeff,
    ocean_mask,
    column_depth,
    east_depth,
    tracers,
    u_clinic,
    v_clinic,
):
    low, high = edge_blocks(column_depth, east_depth, u_clinic, tracers)
    surface, strip, low, high = solve_and_hand_over(
        surface_old, surface_forcing, surface_coeff, ocean_mask, low, high
    )
    edges = ring_of(low, high)
    tracers_new = transport(
        strip, column_depth, east_depth, u_clinic, v_clinic, edges, tracers
    )
    return (surface, tracers_new)


def solution(mesh):
    in_specs = (
        P(("member", "lon"), None),
        P(("member", "lon"), None),
        P("lon", None),
        P("lon", None),
        P("lon", None),
        P("lon", None),
        P("member", None, "lon", None),
        P("member", "lon", None),
        P("member", "lon", None),
    )
    out_specs = (P(("member", "lon"), None), P("member", None, "lon", None))
    return jax.shard_map(body, mesh=mesh, in_specs=in_specs, out_specs=out_specs, check_vma=False)
```

```python
import jax
import jax.numpy as jnp
from jax import lax
from jax.experimental import pallas as pl
from jax.experimental.pallas import tpu as pltpu
from jax.sharding import PartitionSpec as P

SOLVER_ITERS = 4
TRACERS = 8


BARO_GAIN = 0.1
HORIZ_DIFF = 0.1
VERT_DIFF = 0.15
RATE_CARBON = 0.3
RATE_AMMONIUM = 0.2
RATE_NITRITE = 0.2
RATE_SULFIDE = 0.3
RATE_NITROUS = 0.2
HALF_OXYGEN = 0.3
HALF_NITRATE = 0.3
HALF_NITRITE = 0.3
YIELD_NITROUS = 0.3


HALO = 8
CENTER = 4.55
HALF_WIDTH = 4.45
LANES = 128
RING = 24
WIDTH = 16
SUM_ROW = WIDTH + 1


def apply_extended(values_in, mask_float, diagonal):
    masked = mask_float * values_in
    total, columns = masked.shape
    northern = pltpu.roll(masked, total - 1, 0)
    southern = pltpu.roll(masked, 1, 0)
    eastern = pltpu.roll(masked, columns - 1, 1)
    western = pltpu.roll(masked, 1, 1)
    return diagonal * values_in - mask_float * (northern + southern + eastern + western)


def krylov_basis(right_side, coeff, mask_float):
    diagonal = (coeff + 4.0 * mask_float) - CENTER
    basis = [right_side]
    for order in range(SOLVER_ITERS):
        now = basis[-1]
        image = apply_extended(now, mask_float, diagonal) * (1.0 / HALF_WIDTH)
        basis.append(image if order == 0 else 2.0 * image - basis[-2])
    return [field[HALO:-HALO] for field in basis]


def reversed_both(block):
    for axis in range(2):
        size = block.shape[axis]
        index = lax.broadcasted_iota(jnp.int32, block.shape, axis)
        bit = 1
        while bit < size:
            up = pltpu.roll(block, size - bit, axis)
            down = pltpu.roll(block, bit, axis)
            block = jnp.where((index // bit) % 2 == 0, up, down)
            bit *= 2
    return block


GRAM_PAIRS = [(i, j) for i in range(SOLVER_ITERS) for j in range(i, SOLVER_ITERS + 1)]


def operator_on_coefficients(given):
    out = [CENTER * value for value in given] + [0.0]
    for k, value in enumerate(given):
        if k == 0:
            out[1] = out[1] + HALF_WIDTH * value
        else:
            out[k - 1] = out[k - 1] + 0.5 * HALF_WIDTH * value
            out[k + 1] = out[k + 1] + 0.5 * HALF_WIDTH * value
    return out


def gram_product(gram, left, right):
    total = 0.0
    for i, x in enumerate(left):
        for j, y in enumerate(right):
            total = total + gram[(min(i, j), max(i, j))] * (x * y)
    return total


def added(first, second):
    size = max(len(first), len(second))
    first = list(first) + [0.0] * (size - len(first))
    second = list(second) + [0.0] * (size - len(second))
    return [x + y for x, y in zip(first, second)]


def solver_coefficients(gram):
    one = gram[(0, 0)] * 0.0 + 1.0
    solution, residual, direction = [], [one], [one]
    norm_now = gram[(0, 0)]
    for sweep in range(SOLVER_ITERS):
        applied = operator_on_coefficients(direction)
        step_size = norm_now / gram_product(gram, direction, applied)
        solution = added(solution, [step_size * x for x in direction])
        if sweep == SOLVER_ITERS - 1:
            break
        residual = added(residual, [-step_size * x for x in applied])
        norm_next = gram_product(gram, residual, residual)
        ratio = norm_next / norm_now
        direction = added(residual, [ratio * x for x in direction])
        norm_now = norm_next
    return solution


def solve_kernel(
    old_ref, forcing_ref, coeff_ref, mask_ref, depth_ref, tracers_ref, low_ref, high_ref,
    surface_ref, strip_ref, partial_ref, low_out, high_out,
    fields, below_in, above_in, send, recv, basis_kept,
    edge_sems, band_sems, send_sems, recv_sems,
):
    count = lax.axis_size("lon")
    me = lax.axis_index("lon")
    right, left = lax.rem(me + 1, count), lax.rem(me + count - 1, count)
    rows, columns = old_ref.shape
    mesh_id = pl.DeviceIdType.MESH

    barrier = pltpu.get_barrier_semaphore()

    def greet(step, carry):
        other = lax.rem(me + step, count)
        pl.semaphore_signal(barrier, inc=1, device_id={"lon": other}, device_id_type=mesh_id)
        return carry

    lax.fori_loop(1, count, greet, 0)
    fields[0] = coeff_ref[...] * old_ref[...] + forcing_ref[...]
    fields[1] = coeff_ref[...]
    fields[2] = mask_ref[...].astype(jnp.float32)
    pl.semaphore_wait(barrier, count - 1)

    def remote(source, target, sems, n, device):
        return pltpu.make_async_remote_copy(
            src_ref=source,
            dst_ref=target,
            send_sem=sems.at[n, 0],
            recv_sem=sems.at[n, 1],
            device_id={"lon": device},
            device_id_type=mesh_id,
        )

    copies = [
        remote(fields.at[:, rows - HALO :], below_in, band_sems, 0, right),
        remote(fields.at[:, :HALO], above_in, band_sems, 1, left),
        remote(low_ref, low_out, edge_sems, 0, right),
        remote(high_ref, high_out, edge_sems, 1, left),
    ]
    for copy in copies:
        copy.start()
    mirrored = [reversed_both(fields[n, rows - HALO :]) for n in range(3)]
    copies[0].wait()
    copies[1].wait()
    bottom = me == 0
    top = me == count - 1
    extended = [
        jnp.concatenate(
            [
                jnp.where(bottom, 0.0, below_in[n]),
                fields[n],
                jnp.where(top, mirrored[n], above_in[n]),
            ],
            axis=0,
        )
        for n in range(3)
    ]
    basis = krylov_basis(*extended)
    lane = lax.broadcasted_iota(jnp.int32, (1, LANES), 1)
    sums = jnp.zeros((1, LANES), jnp.float32)
    for n, (i, j) in enumerate(GRAM_PAIRS):
        total = jnp.sum(jnp.sum(basis[i] * basis[j], axis=0, keepdims=True), axis=1, keepdims=True)
        sums = jnp.where(lane == n, total, sums)
    for k in range(SOLVER_ITERS):
        basis_kept[k] = basis[k]
    tall = jnp.concatenate(basis[:SOLVER_ITERS] * (LANES // (SOLVER_ITERS * rows)), axis=0)
    turned = jnp.transpose(tall)
    row = lax.broadcasted_iota(jnp.int32, (RING - WIDTH, LANES), 0)
    for d in range(count):
        send[d, :WIDTH] = turned[d * WIDTH : (d + 1) * WIDTH]
        after = (d + 1) % count * WIDTH
        before = (d * WIDTH - 8) % columns
        tail = jnp.where(row == SUM_ROW - WIDTH, sums, turned[after : after + 8])
        send[d, WIDTH:] = jnp.where(row == 7, turned[before : before + 8], tail)

    def block_copy(step):
        other = lax.rem(me + step, count)
        return pltpu.make_async_remote_copy(
            src_ref=send.at[other],
            dst_ref=recv.at[me],
            send_sem=send_sems.at[step],
            recv_sem=recv_sems.at[step],
            device_id={"lon": other},
            device_id_type=mesh_id,
        )

    def start_block(step, carry):
        block_copy(step).start()
        return carry

    def wait_block(step, carry):
        block_copy(step).wait()
        return carry

    lax.fori_loop(1, count, start_block, 0)
    recv[me] = send[me]
    column_terms(depth_ref, tracers_ref, partial_ref)
    lax.fori_loop(1, count, wait_block, 0)
    combine(recv, basis_kept, surface_ref, strip_ref)
    copies[2].wait()
    copies[3].wait()


def column_terms(depth_ref, tracers_ref, partial_ref):
    levels = tracers_ref.shape[1]

    def one_level(z, carry):
        depth = depth_ref[...]
        is_wet = depth > z
        wet = is_wet.astype(jnp.float32)
        below = depth > z + 1
        above = jnp.logical_and(is_wet, z > 0)
        z_down = jnp.minimum(z + 1, levels - 1)
        z_up = jnp.maximum(z - 1, 0)
        sources = redox_sources([tracers_ref[k, z] * wet for k in range(TRACERS)])
        for k in range(TRACERS):
            raw = tracers_ref[k, z]
            down = jnp.where(below, tracers_ref[k, z_down] - raw, 0.0)
            up = jnp.where(above, raw - tracers_ref[k, z_up], 0.0)
            partial_ref[k, z] = raw + wet * (VERT_DIFF * (down - up) + sources[k])
        return carry

    lax.fori_loop(0, levels, one_level, 0)


def solve_and_hand_over(
    surface_old, surface_forcing, surface_coeff, ocean_mask, column_depth, tracers, low, high
):
    rows, columns = surface_old.shape
    count = lax.axis_size("lon")
    vmem = pl.BlockSpec(memory_space=pltpu.VMEM)
    anywhere = pl.BlockSpec(memory_space=pl.ANY)
    return pl.pallas_call(
        solve_kernel,
        in_specs=[vmem] * 6 + [anywhere] * 2,
        out_specs=[vmem] * 3 + [anywhere] * 2,
        out_shape=(
            jax.ShapeDtypeStruct((rows, columns), jnp.float32),
            jax.ShapeDtypeStruct((RING, rows * count), jnp.float32),
            jax.ShapeDtypeStruct(tracers.shape, jnp.float32),
            jax.ShapeDtypeStruct(low.shape, jnp.float32),
            jax.ShapeDtypeStruct(high.shape, jnp.float32),
        ),
        scratch_shapes=[
            pltpu.VMEM((3, rows, columns), jnp.float32),
            pltpu.VMEM((3, HALO, columns), jnp.float32),
            pltpu.VMEM((3, HALO, columns), jnp.float32),
            pltpu.VMEM((count, RING, LANES), jnp.float32),
            pltpu.VMEM((count, RING, LANES), jnp.float32),
            pltpu.VMEM((SOLVER_ITERS, rows, columns), jnp.float32),
            pltpu.SemaphoreType.DMA((2, 2)),
            pltpu.SemaphoreType.DMA((2, 2)),
            pltpu.SemaphoreType.DMA((count,)),
            pltpu.SemaphoreType.DMA((count,)),
        ],
        compiler_params=pltpu.CompilerParams(
            collective_id=0, has_side_effects=True, vmem_limit_bytes=20 * 2**20
        ),
    )(
        surface_old, surface_forcing, surface_coeff, ocean_mask, column_depth, tracers, low, high
    )


def combine(moved, basis, surface_ref, strip_ref):
    count, rows = moved.shape[0], basis.shape[1]
    totals = moved[0, SUM_ROW : SUM_ROW + 1, :]
    for source in range(1, count):
        totals = totals + moved[source, SUM_ROW : SUM_ROW + 1, :]
    gram = {pair: totals[:, n : n + 1] for n, pair in enumerate(GRAM_PAIRS)}
    weights = solver_coefficients(gram)
    surface_ref[...] = sum(weights[k] * basis[k] for k in range(SOLVER_ITERS))
    lane = lax.broadcasted_iota(jnp.int32, (1, LANES), 1)
    which = (lane // rows) % SOLVER_ITERS
    scale = jnp.zeros((1, LANES), jnp.float32)
    for k in range(SOLVER_ITERS):
        scale = jnp.where(which == k, weights[k], scale)
    slot = jnp.broadcast_to(lane // rows, (RING, LANES))
    per_group = LANES // rows
    for group in range(count // per_group):
        joined = jnp.zeros((RING, LANES), jnp.float32)
        for q in range(per_group):
            scaled = moved[group * per_group + q] * scale
            scaled = scaled + pltpu.roll(scaled, 2 * rows, 1)
            scaled = scaled + pltpu.roll(scaled, rows, 1)
            joined = jnp.where(slot == q, scaled, joined)
        strip_ref[:, group * LANES : (group + 1) * LANES] = joined


def redox_sources(masked):
    oxygen = masked[0]
    nitrate = masked[1]
    nitrite = masked[2]
    ammonium = masked[3]
    carbon = masked[5]
    sulfide = masked[6]
    nitrous = masked[7]
    breakdown = RATE_CARBON * carbon
    with_oxygen = oxygen / (oxygen + HALF_OXYGEN)
    with_nitrate = (1.0 - with_oxygen) * nitrate / (nitrate + HALF_NITRATE)
    with_nitrite = (1.0 - with_oxygen - with_nitrate) * nitrite / (nitrite + HALF_NITRITE)
    with_sulfate = 1.0 - with_oxygen - with_nitrate - with_nitrite
    first_nitr = RATE_AMMONIUM * ammonium * with_oxygen
    second_nitr = RATE_NITRITE * nitrite * with_oxygen
    sulfide_ox = RATE_SULFIDE * sulfide * with_oxygen
    return (
        [
            -1.3 * breakdown * with_oxygen
            - 1.5 * first_nitr
            - 0.5 * second_nitr
            - 2.0 * sulfide_ox,
            -0.9 * breakdown * with_nitrate + second_nitr,
            0.9 * breakdown * with_nitrate
            - 0.6 * breakdown * with_nitrite
            + (1.0 - YIELD_NITROUS) * first_nitr
            - second_nitr,
            0.15 * breakdown - first_nitr,
            0.1 * breakdown,
            -breakdown,
            0.5 * breakdown * with_sulfate - sulfide_ox,
            YIELD_NITROUS * first_nitr - RATE_NITROUS * nitrous * (1.0 - with_oxygen),
        ]
    )


def transport_kernel(
    strip_ref, depth_ref, east_depth_ref, u_ref, v_ref, edge_ref, tracers_ref, partial_ref, out_ref
):
    z = pl.program_id(0)
    latitudes = depth_ref.shape[1]
    shape = depth_ref.shape

    def ring(block, shift):
        return pltpu.roll(block, shift % RING, 0)

    def along(block, shift):
        return pltpu.roll(block, shift % latitudes, 1)

    column = lax.broadcasted_iota(jnp.int32, shape, 1)
    depth = depth_ref[...]
    wet = (depth > z).astype(jnp.float32)
    strip = strip_ref[...]
    own = strip[: shape[0]]
    flow_edge = edge_ref[TRACERS, 0]
    east_depth = jnp.concatenate(
        [east_depth_ref[...].astype(jnp.float32), ring_edge(flow_edge)], axis=0
    )
    east_open = (east_depth > z.astype(jnp.float32)).astype(jnp.float32)
    u_ext = jnp.concatenate([u_ref[0], flow_edge], axis=0)
    east_flow = (u_ext - BARO_GAIN * (ring(strip, -1) - strip)) * east_open * (1.0 / 12.0)
    east_mix = HORIZ_DIFF * east_open
    last = column == latitudes - 1
    north_open = jnp.where(last, 0.0, wet * along(wet, -1))
    north_flow = (v_ref[0] - BARO_GAIN * (along(own, -1) - own)) * north_open * (1.0 / 12.0)
    north_mix = HORIZ_DIFF * north_open
    first = column == 0

    for k in range(TRACERS):
        masked = tracers_ref[k, 0] * wet
        extended = jnp.concatenate([masked, edge_ref[k, 0]], axis=0)
        east_one = ring(extended, -1)
        pair = extended + east_one
        face = 8.0 * pair - (ring(pair, 1) + ring(pair, -1))
        flux = east_flow * face - east_mix * (east_one - extended)
        change = (ring(flux, 1) - flux)[: shape[0]]
        north_one = jnp.where(last, 0.0, along(masked, -1))
        pair = masked + north_one
        south_pair = jnp.where(first, masked, along(pair, 1))
        north_pair = jnp.where(last, 0.0, along(pair, -1))
        face = 8.0 * pair - (south_pair + north_pair)
        flux = north_flow * face - north_mix * (north_one - masked)
        change = change + (along(flux, 1) - flux)
        out_ref[k, 0] = partial_ref[k, 0] + wet * change


def ring_edge(flow_edge):
    return pltpu.roll(flow_edge, 1, 0)


def transport(strip, column_depth, east_depth, u_clinic, v_clinic, edges, tracers, partial):
    count, levels, width, latitudes = tracers.shape
    whole = lambda shape: pl.BlockSpec(shape, lambda z: (0,) * len(shape))
    level = lambda rows: pl.BlockSpec((1, rows, latitudes), lambda z: (z, 0, 0))
    cut = pl.BlockSpec((count, 1, width, latitudes), lambda z: (0, z, 0, 0))
    return pl.pallas_call(
        transport_kernel,
        grid=(levels,),
        in_specs=[
            whole(strip.shape),
            whole(column_depth.shape),
            whole(east_depth.shape),
            level(width),
            level(width),
            pl.BlockSpec((count + 1, 1, RING - width, latitudes), lambda z: (0, z, 0, 0)),
            cut,
            cut,
        ],
        out_specs=cut,
        out_shape=jax.ShapeDtypeStruct(tracers.shape, jnp.float32),
        compiler_params=pltpu.CompilerParams(vmem_limit_bytes=40 * 2**20),
    )(strip, column_depth, east_depth, u_clinic, v_clinic, edges, tracers, partial)


def edge_blocks(column_depth, east_depth, u_clinic, tracers):
    levels = tracers.shape[1]
    index = lax.broadcasted_iota(jnp.int32, (levels, 1, 1), 0)

    def masked(where):
        wet = index < column_depth[None, where]
        return jnp.where(wet[None], tracers[:, :, where], 0.0)

    ends = jnp.broadcast_to(east_depth[None, -1:].astype(jnp.float32), u_clinic[:, -1:].shape)
    flow = jnp.concatenate([ends, u_clinic[:, -1:]], axis=1)
    low = jnp.concatenate([masked(slice(-2, None)), flow[None]], axis=0)
    return low, masked(slice(0, 2))


def ring_of(low, high):
    high = jnp.pad(high, ((0, 1), (0, 0), (0, RING - WIDTH - 4), (0, 0)))
    return jnp.concatenate([high, low], axis=2)


def body(
    surface_old,
    surface_forcing,
    surface_coeff,
    ocean_mask,
    column_depth,
    east_depth,
    tracers,
    u_clinic,
    v_clinic,
):
    low, high = edge_blocks(column_depth, east_depth, u_clinic, tracers)
    surface, strip, partial, low, high = solve_and_hand_over(
        surface_old, surface_forcing, surface_coeff, ocean_mask, column_depth, tracers, low, high
    )
    edges = ring_of(low, high)
    tracers_new = transport(
        strip, column_depth, east_depth, u_clinic, v_clinic, edges, tracers, partial
    )
    return (surface, tracers_new)


def solution(mesh):
    in_specs = (
        P(("member", "lon"), None),
        P(("member", "lon"), None),
        P("lon", None),
        P("lon", None),
        P("lon", None),
        P("lon", None),
        P("member", None, "lon", None),
        P("member", "lon", None),
        P("member", "lon", None),
    )
    out_specs = (P(("member", "lon"), None), P("member", None, "lon", None))
    return jax.shard_map(body, mesh=mesh, in_specs=in_specs, out_specs=out_specs, check_vma=False)
```

```python
import jax
import jax.numpy as jnp
from jax import lax
from jax.experimental import pallas as pl
from jax.experimental.pallas import tpu as pltpu
from jax.sharding import PartitionSpec as P

SOLVER_ITERS = 4
TRACERS = 8


BARO_GAIN = 0.1
HORIZ_DIFF = 0.1
VERT_DIFF = 0.15
RATE_CARBON = 0.3
RATE_AMMONIUM = 0.2
RATE_NITRITE = 0.2
RATE_SULFIDE = 0.3
RATE_NITROUS = 0.2
HALF_OXYGEN = 0.3
HALF_NITRATE = 0.3
HALF_NITRITE = 0.3
YIELD_NITROUS = 0.3


HALO = 8
CENTER = 4.55
HALF_WIDTH = 4.45
LANES = 128
RING = 24
WIDTH = 16
SUM_ROW = WIDTH + 1


def apply_extended(values_in, mask_float, diagonal):
    masked = mask_float * values_in
    total, columns = masked.shape
    northern = pltpu.roll(masked, total - 1, 0)
    southern = pltpu.roll(masked, 1, 0)
    eastern = pltpu.roll(masked, columns - 1, 1)
    western = pltpu.roll(masked, 1, 1)
    return diagonal * values_in - mask_float * (northern + southern + eastern + western)


def krylov_basis(right_side, coeff, mask_float):
    diagonal = (coeff + 4.0 * mask_float) - CENTER
    basis = [right_side]
    for order in range(SOLVER_ITERS):
        now = basis[-1]
        image = apply_extended(now, mask_float, diagonal) * (1.0 / HALF_WIDTH)
        basis.append(image if order == 0 else 2.0 * image - basis[-2])
    return [field[HALO:-HALO] for field in basis]


def reversed_both(block):
    for axis in range(2):
        size = block.shape[axis]
        index = lax.broadcasted_iota(jnp.int32, block.shape, axis)
        bit = 1
        while bit < size:
            up = pltpu.roll(block, size - bit, axis)
            down = pltpu.roll(block, bit, axis)
            block = jnp.where((index // bit) % 2 == 0, up, down)
            bit *= 2
    return block


GRAM_PAIRS = [(i, j) for i in range(SOLVER_ITERS) for j in range(i, SOLVER_ITERS + 1)]


def operator_on_coefficients(given):
    out = [CENTER * value for value in given] + [0.0]
    for k, value in enumerate(given):
        if k == 0:
            out[1] = out[1] + HALF_WIDTH * value
        else:
            out[k - 1] = out[k - 1] + 0.5 * HALF_WIDTH * value
            out[k + 1] = out[k + 1] + 0.5 * HALF_WIDTH * value
    return out


def gram_product(gram, left, right):
    total = 0.0
    for i, x in enumerate(left):
        for j, y in enumerate(right):
            total = total + gram[(min(i, j), max(i, j))] * (x * y)
    return total


def added(first, second):
    size = max(len(first), len(second))
    first = list(first) + [0.0] * (size - len(first))
    second = list(second) + [0.0] * (size - len(second))
    return [x + y for x, y in zip(first, second)]


def solver_coefficients(gram):
    one = gram[(0, 0)] * 0.0 + 1.0
    solution, residual, direction = [], [one], [one]
    norm_now = gram[(0, 0)]
    for sweep in range(SOLVER_ITERS):
        applied = operator_on_coefficients(direction)
        step_size = norm_now / gram_product(gram, direction, applied)
        solution = added(solution, [step_size * x for x in direction])
        if sweep == SOLVER_ITERS - 1:
            break
        residual = added(residual, [-step_size * x for x in applied])
        norm_next = gram_product(gram, residual, residual)
        ratio = norm_next / norm_now
        direction = added(residual, [ratio * x for x in direction])
        norm_now = norm_next
    return solution


def solve_kernel(
    old_ref, forcing_ref, coeff_ref, mask_ref, depth_ref, tracers_hbm, v_hbm, low_ref, high_ref,
    surface_ref, strip_ref, partial_ref, low_out, high_out,
    fields, below_in, above_in, send, recv, basis_kept, tracers_ref, v_ref,
    edge_sems, band_sems, send_sems, recv_sems, local_sems,
):
    count = lax.axis_size("lon")
    me = lax.axis_index("lon")
    right, left = lax.rem(me + 1, count), lax.rem(me + count - 1, count)
    rows, columns = old_ref.shape
    mesh_id = pl.DeviceIdType.MESH

    barrier = pltpu.get_barrier_semaphore()

    def greet(step, carry):
        other = lax.rem(me + step, count)
        pl.semaphore_signal(barrier, inc=1, device_id={"lon": other}, device_id_type=mesh_id)
        return carry

    lax.fori_loop(1, count, greet, 0)
    fetches = [
        pltpu.make_async_copy(tracers_hbm, tracers_ref, local_sems.at[0]),
        pltpu.make_async_copy(v_hbm, v_ref, local_sems.at[1]),
    ]
    for fetch in fetches:
        fetch.start()
    fields[0] = coeff_ref[...] * old_ref[...] + forcing_ref[...]
    fields[1] = coeff_ref[...]
    fields[2] = mask_ref[...].astype(jnp.float32)
    pl.semaphore_wait(barrier, count - 1)

    def remote(source, target, sems, n, device):
        return pltpu.make_async_remote_copy(
            src_ref=source,
            dst_ref=target,
            send_sem=sems.at[n, 0],
            recv_sem=sems.at[n, 1],
            device_id={"lon": device},
            device_id_type=mesh_id,
        )

    copies = [
        remote(fields.at[:, rows - HALO :], below_in, band_sems, 0, right),
        remote(fields.at[:, :HALO], above_in, band_sems, 1, left),
        remote(low_ref, low_out, edge_sems, 0, right),
        remote(high_ref, high_out, edge_sems, 1, left),
    ]
    for copy in copies:
        copy.start()
    mirrored = [reversed_both(fields[n, rows - HALO :]) for n in range(3)]
    copies[0].wait()
    copies[1].wait()
    bottom = me == 0
    top = me == count - 1
    extended = [
        jnp.concatenate(
            [
                jnp.where(bottom, 0.0, below_in[n]),
                fields[n],
                jnp.where(top, mirrored[n], above_in[n]),
            ],
            axis=0,
        )
        for n in range(3)
    ]
    basis = krylov_basis(*extended)
    lane = lax.broadcasted_iota(jnp.int32, (1, LANES), 1)
    sums = jnp.zeros((1, LANES), jnp.float32)
    for n, (i, j) in enumerate(GRAM_PAIRS):
        total = jnp.sum(jnp.sum(basis[i] * basis[j], axis=0, keepdims=True), axis=1, keepdims=True)
        sums = jnp.where(lane == n, total, sums)
    for k in range(SOLVER_ITERS):
        basis_kept[k] = basis[k]
    tall = jnp.concatenate(basis[:SOLVER_ITERS] * (LANES // (SOLVER_ITERS * rows)), axis=0)
    turned = jnp.transpose(tall)
    row = lax.broadcasted_iota(jnp.int32, (RING - WIDTH, LANES), 0)
    for d in range(count):
        send[d, :WIDTH] = turned[d * WIDTH : (d + 1) * WIDTH]
        after = (d + 1) % count * WIDTH
        before = (d * WIDTH - 8) % columns
        tail = jnp.where(row == SUM_ROW - WIDTH, sums, turned[after : after + 8])
        send[d, WIDTH:] = jnp.where(row == 7, turned[before : before + 8], tail)

    def block_copy(step):
        other = lax.rem(me + step, count)
        return pltpu.make_async_remote_copy(
            src_ref=send.at[other],
            dst_ref=recv.at[me],
            send_sem=send_sems.at[step],
            recv_sem=recv_sems.at[step],
            device_id={"lon": other},
            device_id_type=mesh_id,
        )

    def start_block(step, carry):
        block_copy(step).start()
        return carry

    def wait_block(step, carry):
        block_copy(step).wait()
        return carry

    lax.fori_loop(1, count, start_block, 0)
    recv[me] = send[me]
    fetches[0].wait()
    fetches[1].wait()
    column_terms(depth_ref, tracers_ref, partial_ref)
    lax.fori_loop(1, count, wait_block, 0)
    combine(recv, basis_kept, surface_ref, strip_ref)
    north_terms(strip_ref, depth_ref, v_ref, tracers_ref, partial_ref)
    copies[2].wait()
    copies[3].wait()


def column_terms(depth_ref, tracers_ref, partial_ref):
    levels = tracers_ref.shape[1]

    def one_level(z, carry):
        depth = depth_ref[...]
        is_wet = depth > z
        wet = is_wet.astype(jnp.float32)
        below = depth > z + 1
        above = jnp.logical_and(is_wet, z > 0)
        z_down = jnp.minimum(z + 1, levels - 1)
        z_up = jnp.maximum(z - 1, 0)
        sources = redox_sources([tracers_ref[k, z] * wet for k in range(TRACERS)])
        for k in range(TRACERS):
            raw = tracers_ref[k, z]
            down = jnp.where(below, tracers_ref[k, z_down] - raw, 0.0)
            up = jnp.where(above, raw - tracers_ref[k, z_up], 0.0)
            partial_ref[k, z] = raw + wet * (VERT_DIFF * (down - up) + sources[k])
        return carry

    lax.fori_loop(0, levels, one_level, 0)


def north_terms(strip_ref, depth_ref, v_ref, tracers_ref, partial_ref):
    shape = depth_ref.shape
    latitudes = shape[1]

    def along(block, shift):
        return pltpu.roll(block, shift % latitudes, 1)

    def one_level(z, carry):
        column = lax.broadcasted_iota(jnp.int32, shape, 1)
        last = column == latitudes - 1
        first = column == 0
        wet = (depth_ref[...] > z).astype(jnp.float32)
        own = strip_ref[: shape[0]]
        north_open = jnp.where(last, 0.0, wet * along(wet, -1))
        north_flow = (v_ref[z] - BARO_GAIN * (along(own, -1) - own)) * north_open * (1.0 / 12.0)
        north_mix = HORIZ_DIFF * north_open
        for k in range(TRACERS):
            masked = tracers_ref[k, z] * wet
            north_one = jnp.where(last, 0.0, along(masked, -1))
            pair = masked + north_one
            south_pair = jnp.where(first, masked, along(pair, 1))
            north_pair = jnp.where(last, 0.0, along(pair, -1))
            face = 8.0 * pair - (south_pair + north_pair)
            flux = north_flow * face - north_mix * (north_one - masked)
            partial_ref[k, z] += wet * (along(flux, 1) - flux)
        return carry

    lax.fori_loop(0, tracers_ref.shape[1], one_level, 0)


def solve_and_hand_over(
    surface_old,
    surface_forcing,
    surface_coeff,
    ocean_mask,
    column_depth,
    tracers,
    v_clinic,
    low,
    high,
):
    rows, columns = surface_old.shape
    count = lax.axis_size("lon")
    vmem = pl.BlockSpec(memory_space=pltpu.VMEM)
    anywhere = pl.BlockSpec(memory_space=pl.ANY)
    return pl.pallas_call(
        solve_kernel,
        in_specs=[vmem] * 5 + [anywhere] * 4,
        out_specs=[vmem] * 3 + [anywhere] * 2,
        out_shape=(
            jax.ShapeDtypeStruct((rows, columns), jnp.float32),
            jax.ShapeDtypeStruct((RING, rows * count), jnp.float32),
            jax.ShapeDtypeStruct(tracers.shape, jnp.float32),
            jax.ShapeDtypeStruct(low.shape, jnp.float32),
            jax.ShapeDtypeStruct(high.shape, jnp.float32),
        ),
        scratch_shapes=[
            pltpu.VMEM((3, rows, columns), jnp.float32),
            pltpu.VMEM((3, HALO, columns), jnp.float32),
            pltpu.VMEM((3, HALO, columns), jnp.float32),
            pltpu.VMEM((count, RING, LANES), jnp.float32),
            pltpu.VMEM((count, RING, LANES), jnp.float32),
            pltpu.VMEM((SOLVER_ITERS, rows, columns), jnp.float32),
            pltpu.VMEM(tracers.shape, jnp.float32),
            pltpu.VMEM(v_clinic.shape, jnp.float32),
            pltpu.SemaphoreType.DMA((2, 2)),
            pltpu.SemaphoreType.DMA((2, 2)),
            pltpu.SemaphoreType.DMA((count,)),
            pltpu.SemaphoreType.DMA((count,)),
            pltpu.SemaphoreType.DMA((2,)),
        ],
        compiler_params=pltpu.CompilerParams(
            collective_id=0, has_side_effects=True, vmem_limit_bytes=24 * 2**20
        ),
    )(
        surface_old,
        surface_forcing,
        surface_coeff,
        ocean_mask,
        column_depth,
        tracers,
        v_clinic,
        low,
        high,
    )


def combine(moved, basis, surface_ref, strip_ref):
    count, rows = moved.shape[0], basis.shape[1]
    totals = moved[0, SUM_ROW : SUM_ROW + 1, :]
    for source in range(1, count):
        totals = totals + moved[source, SUM_ROW : SUM_ROW + 1, :]
    gram = {pair: totals[:, n : n + 1] for n, pair in enumerate(GRAM_PAIRS)}
    weights = solver_coefficients(gram)
    surface_ref[...] = sum(weights[k] * basis[k] for k in range(SOLVER_ITERS))
    lane = lax.broadcasted_iota(jnp.int32, (1, LANES), 1)
    which = (lane // rows) % SOLVER_ITERS
    scale = jnp.zeros((1, LANES), jnp.float32)
    for k in range(SOLVER_ITERS):
        scale = jnp.where(which == k, weights[k], scale)
    slot = jnp.broadcast_to(lane // rows, (RING, LANES))
    per_group = LANES // rows
    for group in range(count // per_group):
        joined = jnp.zeros((RING, LANES), jnp.float32)
        for q in range(per_group):
            scaled = moved[group * per_group + q] * scale
            scaled = scaled + pltpu.roll(scaled, 2 * rows, 1)
            scaled = scaled + pltpu.roll(scaled, rows, 1)
            joined = jnp.where(slot == q, scaled, joined)
        strip_ref[:, group * LANES : (group + 1) * LANES] = joined


def redox_sources(masked):
    oxygen = masked[0]
    nitrate = masked[1]
    nitrite = masked[2]
    ammonium = masked[3]
    carbon = masked[5]
    sulfide = masked[6]
    nitrous = masked[7]
    breakdown = RATE_CARBON * carbon
    with_oxygen = oxygen / (oxygen + HALF_OXYGEN)
    with_nitrate = (1.0 - with_oxygen) * nitrate / (nitrate + HALF_NITRATE)
    with_nitrite = (1.0 - with_oxygen - with_nitrate) * nitrite / (nitrite + HALF_NITRITE)
    with_sulfate = 1.0 - with_oxygen - with_nitrate - with_nitrite
    first_nitr = RATE_AMMONIUM * ammonium * with_oxygen
    second_nitr = RATE_NITRITE * nitrite * with_oxygen
    sulfide_ox = RATE_SULFIDE * sulfide * with_oxygen
    return (
        [
            -1.3 * breakdown * with_oxygen
            - 1.5 * first_nitr
            - 0.5 * second_nitr
            - 2.0 * sulfide_ox,
            -0.9 * breakdown * with_nitrate + second_nitr,
            0.9 * breakdown * with_nitrate
            - 0.6 * breakdown * with_nitrite
            + (1.0 - YIELD_NITROUS) * first_nitr
            - second_nitr,
            0.15 * breakdown - first_nitr,
            0.1 * breakdown,
            -breakdown,
            0.5 * breakdown * with_sulfate - sulfide_ox,
            YIELD_NITROUS * first_nitr - RATE_NITROUS * nitrous * (1.0 - with_oxygen),
        ]
    )


def transport_kernel(
    strip_ref, depth_ref, east_depth_ref, u_ref, edge_ref, tracers_ref, partial_ref, out_ref
):
    z = pl.program_id(0)
    shape = depth_ref.shape

    def ring(block, shift):
        return pltpu.roll(block, shift % RING, 0)

    depth = depth_ref[...]
    wet = (depth > z).astype(jnp.float32)
    strip = strip_ref[...]
    flow_edge = edge_ref[TRACERS, 0]
    east_depth = jnp.concatenate(
        [east_depth_ref[...].astype(jnp.float32), ring_edge(flow_edge)], axis=0
    )
    east_open = (east_depth > z.astype(jnp.float32)).astype(jnp.float32)
    u_ext = jnp.concatenate([u_ref[0], flow_edge], axis=0)
    east_flow = (u_ext - BARO_GAIN * (ring(strip, -1) - strip)) * east_open * (1.0 / 12.0)
    east_mix = HORIZ_DIFF * east_open
    for k in range(TRACERS):
        masked = tracers_ref[k, 0] * wet
        extended = jnp.concatenate([masked, edge_ref[k, 0]], axis=0)
        east_one = ring(extended, -1)
        pair = extended + east_one
        face = 8.0 * pair - (ring(pair, 1) + ring(pair, -1))
        flux = east_flow * face - east_mix * (east_one - extended)
        change = (ring(flux, 1) - flux)[: shape[0]]
        out_ref[k, 0] = partial_ref[k, 0] + wet * change


def ring_edge(flow_edge):
    return pltpu.roll(flow_edge, 1, 0)


def transport(strip, column_depth, east_depth, u_clinic, edges, tracers, partial):
    count, levels, width, latitudes = tracers.shape
    whole = lambda shape: pl.BlockSpec(shape, lambda z: (0,) * len(shape))
    level = lambda rows: pl.BlockSpec((1, rows, latitudes), lambda z: (z, 0, 0))
    cut = pl.BlockSpec((count, 1, width, latitudes), lambda z: (0, z, 0, 0))
    return pl.pallas_call(
        transport_kernel,
        grid=(levels,),
        in_specs=[
            whole(strip.shape),
            whole(column_depth.shape),
            whole(east_depth.shape),
            level(width),
            pl.BlockSpec((count + 1, 1, RING - width, latitudes), lambda z: (0, z, 0, 0)),
            cut,
            cut,
        ],
        out_specs=cut,
        out_shape=jax.ShapeDtypeStruct(tracers.shape, jnp.float32),
        compiler_params=pltpu.CompilerParams(vmem_limit_bytes=40 * 2**20),
    )(strip, column_depth, east_depth, u_clinic, edges, tracers, partial)


def edge_blocks(column_depth, east_depth, u_clinic, tracers):
    levels = tracers.shape[1]
    index = lax.broadcasted_iota(jnp.int32, (levels, 1, 1), 0)

    def masked(where):
        wet = index < column_depth[None, where]
        return jnp.where(wet[None], tracers[:, :, where], 0.0)

    ends = jnp.broadcast_to(east_depth[None, -1:].astype(jnp.float32), u_clinic[:, -1:].shape)
    flow = jnp.concatenate([ends, u_clinic[:, -1:]], axis=1)
    low = jnp.concatenate([masked(slice(-2, None)), flow[None]], axis=0)
    return low, masked(slice(0, 2))


def ring_of(low, high):
    high = jnp.pad(high, ((0, 1), (0, 0), (0, RING - WIDTH - 4), (0, 0)))
    return jnp.concatenate([high, low], axis=2)


def body(
    surface_old,
    surface_forcing,
    surface_coeff,
    ocean_mask,
    column_depth,
    east_depth,
    tracers,
    u_clinic,
    v_clinic,
):
    low, high = edge_blocks(column_depth, east_depth, u_clinic, tracers)
    surface, strip, partial, low, high = solve_and_hand_over(
        surface_old,
        surface_forcing,
        surface_coeff,
        ocean_mask,
        column_depth,
        tracers,
        v_clinic,
        low,
        high,
    )
    edges = ring_of(low, high)
    tracers_new = transport(
        strip, column_depth, east_depth, u_clinic, edges, tracers, partial
    )
    return (surface, tracers_new)


def solution(mesh):
    in_specs = (
        P(("member", "lon"), None),
        P(("member", "lon"), None),
        P("lon", None),
        P("lon", None),
        P("lon", None),
        P("lon", None),
        P("member", None, "lon", None),
        P("member", "lon", None),
        P("member", "lon", None),
    )
    out_specs = (P(("member", "lon"), None), P("member", None, "lon", None))
    return jax.shard_map(body, mesh=mesh, in_specs=in_specs, out_specs=out_specs, check_vma=False)
```

```python
import jax
import jax.numpy as jnp
from jax import lax
from jax.experimental import pallas as pl
from jax.experimental.pallas import tpu as pltpu
from jax.sharding import PartitionSpec as P

SOLVER_ITERS = 4
TRACERS = 8


BARO_GAIN = 0.1
HORIZ_DIFF = 0.1
VERT_DIFF = 0.15
RATE_CARBON = 0.3
RATE_AMMONIUM = 0.2
RATE_NITRITE = 0.2
RATE_SULFIDE = 0.3
RATE_NITROUS = 0.2
HALF_OXYGEN = 0.3
HALF_NITRATE = 0.3
HALF_NITRITE = 0.3
YIELD_NITROUS = 0.3


HALO = 8
CENTER = 4.55
HALF_WIDTH = 4.45
LANES = 128
RING = 24
WIDTH = 16
SUM_ROW = WIDTH + 1


def apply_extended(values_in, mask_float, diagonal):
    masked = mask_float * values_in
    total, columns = masked.shape
    northern = pltpu.roll(masked, total - 1, 0)
    southern = pltpu.roll(masked, 1, 0)
    eastern = pltpu.roll(masked, columns - 1, 1)
    western = pltpu.roll(masked, 1, 1)
    return diagonal * values_in - mask_float * (northern + southern + eastern + western)


def krylov_basis(right_side, coeff, mask_float):
    diagonal = (coeff + 4.0 * mask_float) - CENTER
    basis = [right_side]
    for order in range(SOLVER_ITERS):
        now = basis[-1]
        image = apply_extended(now, mask_float, diagonal) * (1.0 / HALF_WIDTH)
        basis.append(image if order == 0 else 2.0 * image - basis[-2])
    return [field[HALO:-HALO] for field in basis]


def reversed_both(block):
    for axis in range(2):
        size = block.shape[axis]
        index = lax.broadcasted_iota(jnp.int32, block.shape, axis)
        bit = 1
        while bit < size:
            up = pltpu.roll(block, size - bit, axis)
            down = pltpu.roll(block, bit, axis)
            block = jnp.where((index // bit) % 2 == 0, up, down)
            bit *= 2
    return block


GRAM_PAIRS = [(i, j) for i in range(SOLVER_ITERS) for j in range(i, SOLVER_ITERS + 1)]


def operator_on_coefficients(given):
    out = [CENTER * value for value in given] + [0.0]
    for k, value in enumerate(given):
        if k == 0:
            out[1] = out[1] + HALF_WIDTH * value
        else:
            out[k - 1] = out[k - 1] + 0.5 * HALF_WIDTH * value
            out[k + 1] = out[k + 1] + 0.5 * HALF_WIDTH * value
    return out


def gram_product(gram, left, right):
    total = 0.0
    for i, x in enumerate(left):
        for j, y in enumerate(right):
            total = total + gram[(min(i, j), max(i, j))] * (x * y)
    return total


def added(first, second):
    size = max(len(first), len(second))
    first = list(first) + [0.0] * (size - len(first))
    second = list(second) + [0.0] * (size - len(second))
    return [x + y for x, y in zip(first, second)]


def solver_coefficients(gram):
    one = gram[(0, 0)] * 0.0 + 1.0
    solution, residual, direction = [], [one], [one]
    norm_now = gram[(0, 0)]
    for sweep in range(SOLVER_ITERS):
        applied = operator_on_coefficients(direction)
        step_size = norm_now / gram_product(gram, direction, applied)
        solution = added(solution, [step_size * x for x in direction])
        if sweep == SOLVER_ITERS - 1:
            break
        residual = added(residual, [-step_size * x for x in applied])
        norm_next = gram_product(gram, residual, residual)
        ratio = norm_next / norm_now
        direction = added(residual, [ratio * x for x in direction])
        norm_now = norm_next
    return solution


def solve_kernel(
    old_ref, forcing_ref, coeff_ref, mask_ref, depth_ref, tracers_hbm, low_ref, high_ref,
    surface_ref, strip_ref, partial_ref, low_out, high_out,
    fields, below_in, above_in, send, recv, basis_kept, tracers_ref,
    edge_sems, band_sems, send_sems, recv_sems, local_sem,
):
    count = lax.axis_size("lon")
    me = lax.axis_index("lon")
    right, left = lax.rem(me + 1, count), lax.rem(me + count - 1, count)
    rows, columns = old_ref.shape
    mesh_id = pl.DeviceIdType.MESH

    barrier = pltpu.get_barrier_semaphore()

    def greet(step, carry):
        other = lax.rem(me + step, count)
        pl.semaphore_signal(barrier, inc=1, device_id={"lon": other}, device_id_type=mesh_id)
        return carry

    lax.fori_loop(1, count, greet, 0)
    fetch = pltpu.make_async_copy(tracers_hbm, tracers_ref, local_sem)
    fetch.start()
    fields[0] = coeff_ref[...] * old_ref[...] + forcing_ref[...]
    fields[1] = coeff_ref[...]
    fields[2] = mask_ref[...].astype(jnp.float32)
    pl.semaphore_wait(barrier, count - 1)

    def remote(source, target, sems, n, device):
        return pltpu.make_async_remote_copy(
            src_ref=source,
            dst_ref=target,
            send_sem=sems.at[n, 0],
            recv_sem=sems.at[n, 1],
            device_id={"lon": device},
            device_id_type=mesh_id,
        )

    copies = [
        remote(fields.at[:, rows - HALO :], below_in, band_sems, 0, right),
        remote(fields.at[:, :HALO], above_in, band_sems, 1, left),
        remote(low_ref, low_out, edge_sems, 0, right),
        remote(high_ref, high_out, edge_sems, 1, left),
    ]
    for copy in copies:
        copy.start()
    mirrored = [reversed_both(fields[n, rows - HALO :]) for n in range(3)]
    copies[0].wait()
    copies[1].wait()
    bottom = me == 0
    top = me == count - 1
    extended = [
        jnp.concatenate(
            [
                jnp.where(bottom, 0.0, below_in[n]),
                fields[n],
                jnp.where(top, mirrored[n], above_in[n]),
            ],
            axis=0,
        )
        for n in range(3)
    ]
    basis = krylov_basis(*extended)
    lane = lax.broadcasted_iota(jnp.int32, (1, LANES), 1)
    sums = jnp.zeros((1, LANES), jnp.float32)
    for n, (i, j) in enumerate(GRAM_PAIRS):
        total = jnp.sum(jnp.sum(basis[i] * basis[j], axis=0, keepdims=True), axis=1, keepdims=True)
        sums = jnp.where(lane == n, total, sums)
    for k in range(SOLVER_ITERS):
        basis_kept[k] = basis[k]
    tall = jnp.concatenate(basis[:SOLVER_ITERS] * (LANES // (SOLVER_ITERS * rows)), axis=0)
    turned = jnp.transpose(tall)
    row = lax.broadcasted_iota(jnp.int32, (RING - WIDTH, LANES), 0)
    for d in range(count):
        send[d, :WIDTH] = turned[d * WIDTH : (d + 1) * WIDTH]
        after = (d + 1) % count * WIDTH
        before = (d * WIDTH - 8) % columns
        tail = jnp.where(row == SUM_ROW - WIDTH, sums, turned[after : after + 8])
        send[d, WIDTH:] = jnp.where(row == 7, turned[before : before + 8], tail)

    def block_copy(step):
        other = lax.rem(me + step, count)
        return pltpu.make_async_remote_copy(
            src_ref=send.at[other],
            dst_ref=recv.at[me],
            send_sem=send_sems.at[step],
            recv_sem=recv_sems.at[step],
            device_id={"lon": other},
            device_id_type=mesh_id,
        )

    def start_block(step, carry):
        block_copy(step).start()
        return carry

    def wait_block(step, carry):
        block_copy(step).wait()
        return carry

    lax.fori_loop(1, count, start_block, 0)
    recv[me] = send[me]
    fetch.wait()
    column_terms(depth_ref, tracers_ref, partial_ref)
    lax.fori_loop(1, count, wait_block, 0)
    combine(recv, basis_kept, surface_ref, strip_ref)
    copies[2].wait()
    copies[3].wait()


def column_terms(depth_ref, tracers_ref, partial_ref):
    levels = tracers_ref.shape[1]

    def one_level(z, carry):
        depth = depth_ref[...]
        is_wet = depth > z
        wet = is_wet.astype(jnp.float32)
        below = depth > z + 1
        above = jnp.logical_and(is_wet, z > 0)
        z_down = jnp.minimum(z + 1, levels - 1)
        z_up = jnp.maximum(z - 1, 0)
        sources = redox_sources([tracers_ref[k, z] * wet for k in range(TRACERS)])
        for k in range(TRACERS):
            raw = tracers_ref[k, z]
            down = jnp.where(below, tracers_ref[k, z_down] - raw, 0.0)
            up = jnp.where(above, raw - tracers_ref[k, z_up], 0.0)
            partial_ref[k, z] = raw + wet * (VERT_DIFF * (down - up) + sources[k])
        return carry

    lax.fori_loop(0, levels, one_level, 0)


def solve_and_hand_over(
    surface_old, surface_forcing, surface_coeff, ocean_mask, column_depth, tracers, low, high
):
    rows, columns = surface_old.shape
    count = lax.axis_size("lon")
    vmem = pl.BlockSpec(memory_space=pltpu.VMEM)
    anywhere = pl.BlockSpec(memory_space=pl.ANY)
    return pl.pallas_call(
        solve_kernel,
        in_specs=[vmem] * 5 + [pl.BlockSpec(memory_space=pltpu.HBM)] + [anywhere] * 2,
        out_specs=[vmem] * 3 + [anywhere] * 2,
        out_shape=(
            jax.ShapeDtypeStruct((rows, columns), jnp.float32),
            jax.ShapeDtypeStruct((RING, rows * count), jnp.float32),
            jax.ShapeDtypeStruct(tracers.shape, jnp.float32),
            jax.ShapeDtypeStruct(low.shape, jnp.float32),
            jax.ShapeDtypeStruct(high.shape, jnp.float32),
        ),
        scratch_shapes=[
            pltpu.VMEM((3, rows, columns), jnp.float32),
            pltpu.VMEM((3, HALO, columns), jnp.float32),
            pltpu.VMEM((3, HALO, columns), jnp.float32),
            pltpu.VMEM((count, RING, LANES), jnp.float32),
            pltpu.VMEM((count, RING, LANES), jnp.float32),
            pltpu.VMEM((SOLVER_ITERS, rows, columns), jnp.float32),
            pltpu.VMEM(tracers.shape, jnp.float32),
            pltpu.SemaphoreType.DMA((2, 2)),
            pltpu.SemaphoreType.DMA((2, 2)),
            pltpu.SemaphoreType.DMA((count,)),
            pltpu.SemaphoreType.DMA((count,)),
            pltpu.SemaphoreType.DMA,
        ],
        compiler_params=pltpu.CompilerParams(
            collective_id=0, has_side_effects=True, vmem_limit_bytes=24 * 2**20
        ),
    )(
        surface_old, surface_forcing, surface_coeff, ocean_mask, column_depth, tracers, low, high
    )


def combine(moved, basis, surface_ref, strip_ref):
    count, rows = moved.shape[0], basis.shape[1]
    totals = moved[0, SUM_ROW : SUM_ROW + 1, :]
    for source in range(1, count):
        totals = totals + moved[source, SUM_ROW : SUM_ROW + 1, :]
    gram = {pair: totals[:, n : n + 1] for n, pair in enumerate(GRAM_PAIRS)}
    weights = solver_coefficients(gram)
    surface_ref[...] = sum(weights[k] * basis[k] for k in range(SOLVER_ITERS))
    lane = lax.broadcasted_iota(jnp.int32, (1, LANES), 1)
    which = (lane // rows) % SOLVER_ITERS
    scale = jnp.zeros((1, LANES), jnp.float32)
    for k in range(SOLVER_ITERS):
        scale = jnp.where(which == k, weights[k], scale)
    slot = jnp.broadcast_to(lane // rows, (RING, LANES))
    per_group = LANES // rows
    for group in range(count // per_group):
        joined = jnp.zeros((RING, LANES), jnp.float32)
        for q in range(per_group):
            scaled = moved[group * per_group + q] * scale
            scaled = scaled + pltpu.roll(scaled, 2 * rows, 1)
            scaled = scaled + pltpu.roll(scaled, rows, 1)
            joined = jnp.where(slot == q, scaled, joined)
        strip_ref[:, group * LANES : (group + 1) * LANES] = joined


def redox_sources(masked):
    oxygen = masked[0]
    nitrate = masked[1]
    nitrite = masked[2]
    ammonium = masked[3]
    carbon = masked[5]
    sulfide = masked[6]
    nitrous = masked[7]
    breakdown = RATE_CARBON * carbon
    with_oxygen = oxygen / (oxygen + HALF_OXYGEN)
    with_nitrate = (1.0 - with_oxygen) * nitrate / (nitrate + HALF_NITRATE)
    with_nitrite = (1.0 - with_oxygen - with_nitrate) * nitrite / (nitrite + HALF_NITRITE)
    with_sulfate = 1.0 - with_oxygen - with_nitrate - with_nitrite
    first_nitr = RATE_AMMONIUM * ammonium * with_oxygen
    second_nitr = RATE_NITRITE * nitrite * with_oxygen
    sulfide_ox = RATE_SULFIDE * sulfide * with_oxygen
    return (
        [
            -1.3 * breakdown * with_oxygen
            - 1.5 * first_nitr
            - 0.5 * second_nitr
            - 2.0 * sulfide_ox,
            -0.9 * breakdown * with_nitrate + second_nitr,
            0.9 * breakdown * with_nitrate
            - 0.6 * breakdown * with_nitrite
            + (1.0 - YIELD_NITROUS) * first_nitr
            - second_nitr,
            0.15 * breakdown - first_nitr,
            0.1 * breakdown,
            -breakdown,
            0.5 * breakdown * with_sulfate - sulfide_ox,
            YIELD_NITROUS * first_nitr - RATE_NITROUS * nitrous * (1.0 - with_oxygen),
        ]
    )


def transport_kernel(
    strip_ref, depth_ref, east_depth_ref, u_ref, v_ref, edge_ref, tracers_ref, partial_ref, out_ref
):
    z = pl.program_id(0)
    latitudes = depth_ref.shape[1]
    shape = depth_ref.shape

    def ring(block, shift):
        return pltpu.roll(block, shift % RING, 0)

    def along(block, shift):
        return pltpu.roll(block, shift % latitudes, 1)

    column = lax.broadcasted_iota(jnp.int32, shape, 1)
    depth = depth_ref[...]
    wet = (depth > z).astype(jnp.float32)
    strip = strip_ref[...]
    own = strip[: shape[0]]
    flow_edge = edge_ref[TRACERS, 0]
    east_depth = jnp.concatenate(
        [east_depth_ref[...].astype(jnp.float32), ring_edge(flow_edge)], axis=0
    )
    east_open = (east_depth > z.astype(jnp.float32)).astype(jnp.float32)
    u_ext = jnp.concatenate([u_ref[0], flow_edge], axis=0)
    east_flow = (u_ext - BARO_GAIN * (ring(strip, -1) - strip)) * east_open * (1.0 / 12.0)
    east_mix = HORIZ_DIFF * east_open
    last = column == latitudes - 1
    north_open = jnp.where(last, 0.0, wet * along(wet, -1))
    north_flow = (v_ref[0] - BARO_GAIN * (along(own, -1) - own)) * north_open * (1.0 / 12.0)
    north_mix = HORIZ_DIFF * north_open
    first = column == 0

    for k in range(TRACERS):
        masked = tracers_ref[k, 0] * wet
        extended = jnp.concatenate([masked, edge_ref[k, 0]], axis=0)
        east_one = ring(extended, -1)
        pair = extended + east_one
        face = 8.0 * pair - (ring(pair, 1) + ring(pair, -1))
        flux = east_flow * face - east_mix * (east_one - extended)
        change = (ring(flux, 1) - flux)[: shape[0]]
        north_one = jnp.where(last, 0.0, along(masked, -1))
        pair = masked + north_one
        south_pair = jnp.where(first, masked, along(pair, 1))
        north_pair = jnp.where(last, 0.0, along(pair, -1))
        face = 8.0 * pair - (south_pair + north_pair)
        flux = north_flow * face - north_mix * (north_one - masked)
        change = change + (along(flux, 1) - flux)
        out_ref[k, 0] = partial_ref[k, 0] + wet * change


def ring_edge(flow_edge):
    return pltpu.roll(flow_edge, 1, 0)


def transport(strip, column_depth, east_depth, u_clinic, v_clinic, edges, tracers, partial):
    count, levels, width, latitudes = tracers.shape
    whole = lambda shape: pl.BlockSpec(shape, lambda z: (0,) * len(shape))
    level = lambda rows: pl.BlockSpec((1, rows, latitudes), lambda z: (z, 0, 0))
    cut = pl.BlockSpec((count, 1, width, latitudes), lambda z: (0, z, 0, 0))
    return pl.pallas_call(
        transport_kernel,
        grid=(levels,),
        in_specs=[
            whole(strip.shape),
            whole(column_depth.shape),
            whole(east_depth.shape),
            level(width),
            level(width),
            pl.BlockSpec((count + 1, 1, RING - width, latitudes), lambda z: (0, z, 0, 0)),
            cut,
            cut,
        ],
        out_specs=cut,
        out_shape=jax.ShapeDtypeStruct(tracers.shape, jnp.float32),
        compiler_params=pltpu.CompilerParams(vmem_limit_bytes=40 * 2**20),
    )(strip, column_depth, east_depth, u_clinic, v_clinic, edges, tracers, partial)


def edge_blocks(column_depth, east_depth, u_clinic, tracers):
    levels = tracers.shape[1]
    index = lax.broadcasted_iota(jnp.int32, (levels, 1, 1), 0)

    def masked(where):
        wet = index < column_depth[None, where]
        return jnp.where(wet[None], tracers[:, :, where], 0.0)

    ends = jnp.broadcast_to(east_depth[None, -1:].astype(jnp.float32), u_clinic[:, -1:].shape)
    flow = jnp.concatenate([ends, u_clinic[:, -1:]], axis=1)
    low = jnp.concatenate([masked(slice(-2, None)), flow[None]], axis=0)
    return low, masked(slice(0, 2))


def ring_of(low, high):
    high = jnp.pad(high, ((0, 1), (0, 0), (0, RING - WIDTH - 4), (0, 0)))
    return jnp.concatenate([high, low], axis=2)


def body(
    surface_old,
    surface_forcing,
    surface_coeff,
    ocean_mask,
    column_depth,
    east_depth,
    tracers,
    u_clinic,
    v_clinic,
):
    low, high = edge_blocks(column_depth, east_depth, u_clinic, tracers)
    surface, strip, partial, low, high = solve_and_hand_over(
        surface_old, surface_forcing, surface_coeff, ocean_mask, column_depth, tracers, low, high
    )
    edges = ring_of(low, high)
    tracers_new = transport(
        strip, column_depth, east_depth, u_clinic, v_clinic, edges, tracers, partial
    )
    return (surface, tracers_new)


def solution(mesh):
    in_specs = (
        P(("member", "lon"), None),
        P(("member", "lon"), None),
        P("lon", None),
        P("lon", None),
        P("lon", None),
        P("lon", None),
        P("member", None, "lon", None),
        P("member", "lon", None),
        P("member", "lon", None),
    )
    out_specs = (P(("member", "lon"), None), P("member", None, "lon", None))
    return jax.shard_map(body, mesh=mesh, in_specs=in_specs, out_specs=out_specs, check_vma=False)
```
